32 devices in a mesh: grp: 2 (over y), gx: 4 (over z), yz: 4 (over x, core).
Axes of the slice: x: 2, y: 2, z: 4, core: 2. Of those that a mesh axis runs over, the one named last changes fastest.
Arguments:
- rhs: float32 [12, 16, 8, 512], P('gx', 'yz', 'grp'), may hold values from -5 to 5
- coeff: float32 [12, 16, 8], P('gx', 'yz', 'grp'), may hold values from 0.5 to 2
- flags: int32 [12, 16, 8], P('gx', 'yz', 'grp'), may hold values 0 or 1
- basis: float32 [8, 8], replicated, may hold values from -1 to 1, as said below
- eigenvalues: float32 [8], replicated, may hold values from 0.2 to 4
Outputs:
- solution: float32 [12, 16, 8, 512], P('gx', 'yz', 'grp')
The draws below stay inside these ranges and needn't reach their ends.
Inputs may be any that keep to these rules, and one draw needn't show every extreme that they name: basis is orthogonal: its transpose is its inverse.
All inputs are finite; a program needn't handle non-finite values. No bound on the sum of `flags` on one device may be relied on, other than what follows from the above.
Results may differ from the reference program's by a relative error of at most 0.0003.
Values sent between devices are 32-bit elements; how exact they have to be, the bound alone decides.
A program may use at most 64 MiB of HBM per device.

```python
import math
import jax
import jax.numpy as jnp
import numpy as np
from jax import lax

DEG1 = 8
NODES = 512
ITERS = 2
CHEB = 4
EX = 12
EY = 16
EZ = 8


def draw_rhs(key, part):
    values = jax.random.truncated_normal(key, -5.0, 5.0, (EX, EY, EZ, NODES), jnp.float32)
    return values


def draw_basis(key, part):
    matrix = jax.random.normal(key, (DEG1, DEG1), jnp.float32)
    orthogonal, upper_part = jnp.linalg.qr(matrix)
    return orthogonal


def place_ends(entries, key, least, largest):
    place = [jax.random.randint(jax.random.fold_in(key, axis), (), 0, length) for axis, length in enumerate(entries.shape)]
    main_axis = entries.shape.index(max(entries.shape))
    neighbour = place[:main_axis] + [(place[main_axis] + 1) % entries.shape[main_axis]] + place[main_axis + 1:]
    return entries.at[tuple(place)].set(least).at[tuple(neighbour)].set(largest)


def shard_levels(stream_key, shape, shards, smallest, largest):
    gain = 1.0
    for axis_at, parts in shards:
        steps = jax.random.uniform(jax.random.fold_in(jax.random.fold_in(stream_key, 6), axis_at), (parts,), jnp.float32, smallest / len(shards), largest / len(shards))
        gain = gain * jnp.repeat(jnp.exp(steps), shape[axis_at] // parts).reshape((-1,) + (1,) * (len(shape) - 1 - axis_at))
    return gain


def setup_inputs(seed: int = 0) -> dict:
    seeds = jax.random.split(jax.random.key(seed), 6)
    rhs = draw_rhs(jax.random.fold_in(seeds[5], 71), 0)
    coeff = jnp.clip(jnp.exp(math.log(2.0) - 1.3862944 * jax.random.uniform(seeds[1], (EX, EY, EZ), jnp.float32) ** shard_levels(seeds[1], (EX, EY, EZ), ((0, 4), (1, 4), (2, 2)), -0.2, 0.2)), 0.5, 2.0)
    flags = place_ends((jax.random.randint(seeds[2], (EX, EY, EZ), 0, 2) < 1).astype(jnp.int32), jax.random.fold_in(seeds[2], 1), 0, 1)
    basis = draw_basis(jax.random.fold_in(seeds[5], 71), 0)
    eigenvalues = jnp.clip(jnp.exp(jax.random.uniform(seeds[4], (DEG1,), jnp.float32, math.log(0.2), math.log(4.0))), 0.2, 4.0)
    return {"rhs": rhs, "coeff": coeff, "flags": flags, "basis": basis, "eigenvalues": eigenvalues}


PENALTY = 2.0
COARSE_PENALTY = 1.0
DAMPING = 0.5
CHEB_LOW = 0.1
CHEB_HIGH = 2.0
GLL_POINTS = (-1.0, -0.8717401485096066, -0.5917001814331423, -0.2092992179024789, 0.2092992179024789, 0.5917001814331423, 0.8717401485096066, 1.0)
HIGHEST = lax.Precision.HIGHEST

def build_tables(basis, eigenvalues):
    eigen_table = (basis[:, None, None, :, None, None] * basis[None, :, None, None, :, None] * basis[None, None, :, None, None, :]).reshape(DEG1 ** 3, DEG1 ** 3)
    spectrum = (eigenvalues[:, None, None] + eigenvalues[None, :, None] + eigenvalues[None, None, :]).reshape(-1)
    points = jnp.array(np.array(GLL_POINTS), jnp.float32)
    linear = jnp.stack([(1.0 - points) * 0.5, (1.0 + points) * 0.5])
    restrict_table = (linear.T[:, None, None, :, None, None] * linear.T[None, :, None, None, :, None] * linear.T[None, None, :, None, None, :]).reshape(DEG1 ** 3, 8)
    return (eigen_table, spectrum, restrict_table)

def eigen_apply(values, eigen_table, scale):
    flat = values.reshape(-1, eigen_table.shape[0])
    inside = jnp.dot(flat.astype(jnp.float32), eigen_table.astype(jnp.float32), precision=HIGHEST, preferred_element_type=jnp.float32)
    scaled = inside * scale.reshape(flat.shape)
    back = lax.dot_general(scaled.astype(jnp.float32), eigen_table.astype(jnp.float32), (((1,), (1,)), ((), ())), precision=HIGHEST, preferred_element_type=jnp.float32)
    return back.reshape(values.shape)

def boundary_coefs(flag_values, starts, totals, penalty):
    result_list = []
    for dimension in range(3):
        position = starts[dimension] + lax.broadcasted_iota(jnp.int32, flag_values.shape, dimension)
        lower_coef = penalty * jnp.where(position > 0, 1.0, flag_values)
        upper_coef = penalty * jnp.where(position < totals[dimension] - 1, 1.0, flag_values)
        result_list.append((lower_coef[..., None, None, None], upper_coef[..., None, None, None]))
    return result_list

def neighbour_traces(padded, points):
    lower_list, upper_list = ([], [])
    for dimension in range(3):
        interior = [slice(1, -1)] * 3
        before_index = list(interior)
        before_index[dimension] = slice(0, -2)
        after_index = list(interior)
        after_index[dimension] = slice(2, None)
        lower_list.append(lax.slice_in_dim(padded[tuple(before_index)], points - 1, points, axis=3 + dimension))
        upper_list.append(lax.slice_in_dim(padded[tuple(after_index)], 0, 1, axis=3 + dimension))
    return (lower_list, upper_list)

def face_term(field, lower_list, upper_list, coefs, penalty):
    summed = jnp.zeros_like(field)
    points = field.shape[3]
    for dimension in range(3):
        node_axis = 3 + dimension
        low_face = lax.slice_in_dim(field, 0, 1, axis=node_axis)
        high_face = lax.slice_in_dim(field, points - 1, points, axis=node_axis)
        lower_coef, upper_coef = coefs[dimension]
        low_term = lower_coef * low_face - penalty * lower_list[dimension]
        high_term = upper_coef * high_face - penalty * upper_list[dimension]
        low_pad = [(0, 0)] * 6
        low_pad[node_axis] = (0, points - 1)
        high_pad = [(0, 0)] * 6
        high_pad[node_axis] = (points - 1, 0)
        summed = summed + jnp.pad(low_term, low_pad) + jnp.pad(high_term, high_pad)
    return summed

def coarse_block(corners, coarse_coeff):
    weight = coarse_coeff[..., None, None, None]
    return weight * (3.5 * corners - jnp.flip(corners, 3) - jnp.flip(corners, 4) - jnp.flip(corners, 5))

def chebyshev(coarse_rhs, coarse_coeff, apply_coarse):
    center = 0.5 * (CHEB_HIGH + CHEB_LOW)
    half_width = 0.5 * (CHEB_HIGH - CHEB_LOW)
    sigma_value = center / half_width
    rho_now = 1.0 / sigma_value
    inverse_diag = (1.0 / (coarse_coeff * 3.5 + 3.0 * COARSE_PENALTY))[..., None]
    remain = coarse_rhs
    update = inverse_diag * remain / center
    result = update
    for sweep_num in range(CHEB - 1):
        remain = remain - apply_coarse(update)
        rho_next = 1.0 / (2.0 * sigma_value - rho_now)
        update = rho_next * rho_now * update + 2.0 * rho_next / half_width * (inverse_diag * remain)
        result = result + update
        rho_now = rho_next
    return result

def reference(rhs, coeff, flags, basis, eigenvalues):
    eigen_table, spectrum, restrict_table = build_tables(basis, eigenvalues)
    shape_three = rhs.shape[:3]
    node_count = rhs.shape[3]
    flag_values = flags.astype(jnp.float32)
    fine_coefs = boundary_coefs(flag_values, (0, 0, 0), shape_three, PENALTY)
    coarse_coefs = boundary_coefs(flag_values, (0, 0, 0), shape_three, COARSE_PENALTY)
    block_scale = coeff[..., None] * spectrum
    inverse_scale = 1.0 / block_scale

    def apply_fine(solution):
        field = solution.reshape(shape_three + (DEG1, DEG1, DEG1))
        padded = jnp.pad(field, ((1, 1), (1, 1), (1, 1), (0, 0), (0, 0), (0, 0)))
        lower_list, upper_list = neighbour_traces(padded, DEG1)
        faces = face_term(field, lower_list, upper_list, fine_coefs, PENALTY).reshape(solution.shape)
        return eigen_apply(solution, eigen_table, block_scale) + faces

    def apply_coarse(values):
        corners = values.reshape(values.shape[:3] + (2, 2, 2))
        padded = jnp.pad(corners, ((1, 1), (1, 1), (1, 1), (0, 0), (0, 0), (0, 0)))
        lower_list, upper_list = neighbour_traces(padded, 2)
        faces = face_term(corners, lower_list, upper_list, coarse_coefs, COARSE_PENALTY)
        return (coarse_block(corners, coeff) + faces).reshape(values.shape)
    solution = jnp.zeros_like(rhs)
    for iteration in range(ITERS):
        residual = rhs if iteration == 0 else rhs - apply_fine(solution)
        smoothed = eigen_apply(residual, eigen_table, inverse_scale)
        coarse_rhs = jnp.dot(residual.reshape(-1, node_count).astype(jnp.float32), restrict_table.astype(jnp.float32), precision=HIGHEST, preferred_element_type=jnp.float32).reshape(shape_three + (8,))
        coarse_sol = chebyshev(coarse_rhs, coeff, apply_coarse)
        lifted = lax.dot_general(coarse_sol.reshape(-1, 8).astype(jnp.float32), restrict_table.astype(jnp.float32), (((1,), (1,)), ((), ())), precision=HIGHEST, preferred_element_type=jnp.float32).reshape(rhs.shape)
        solution = solution + DAMPING * (smoothed + lifted)
    return solution
```

```python
import functools

import jax
import jax.numpy as jnp
import numpy as np
from jax import lax
from jax.experimental import pallas as pl
from jax.experimental.pallas import tpu as pltpu
from jax.sharding import PartitionSpec as P

DEG1 = 8
NODES = 512
CHEB = 4
CHEB_LOW = 0.1
CHEB_HIGH = 2.0
REACH = 7
REACH_FACE = 4
GLL_POINTS = (
    -1.0,
    -0.8717401485096066,
    -0.5917001814331423,
    -0.2092992179024789,
    0.2092992179024789,
    0.5917001814331423,
    0.8717401485096066,
    1.0,
)
L0 = [(1.0 - x) * 0.5 for x in GLL_POINTS]
L1 = [(1.0 + x) * 0.5 for x in GLL_POINTS]
MASS_SAME = sum(a * a for a in L0)
MASS_OTHER = sum(a * b for a, b in zip(L0, L1))
HIGHEST = lax.Precision.HIGHEST
MESH = pl.DeviceIdType.MESH
F32 = jnp.float32
BF16 = jnp.bfloat16


def iota(shape, dim):
    return lax.broadcasted_iota(jnp.int32, shape, dim)


def dot(a, b, dims=((1,), (0,))):
    return lax.dot_general(a, b, (dims, ((), ())), precision=HIGHEST, preferred_element_type=F32)


def split(x):
    hi = x.astype(BF16)
    return hi, (x - hi.astype(F32)).astype(BF16)


def dot3(x, hi, lo):
    xh, xl = split(x)
    d = functools.partial(jnp.dot, preferred_element_type=F32)
    return d(xh, hi) + (d(xl, hi) + d(xh, lo))


def pick(index, table):
    out = jnp.full(index.shape, table[0], F32)
    for i in range(1, len(table)):
        out = jnp.where(index == i, table[i], out)
    return out


def offsets(reach):
    return [k for r in range(1, reach + 1) for k in (-r, r)]


def kernel(
    cfg,
    rhs_ref, coeff_ref, flags_ref, basis_ref, eig_ref,
    out_ref,
    mine, other, win, planes, cfx, ext3, ext1,
    rhs_s, s_ref, e_hi, e_lo, t_hi, t_lo,
    ysend, yrecv, zsend, zrecv, xrecv, nb,
    send_sem, recv_sem, fsend, frecv,
):
    n_grp, n_gx, n_yz, LX, LY, LZ, WG, WH, RG, RH, RGF, RHF = cfg
    LT = planes.shape[0]
    L = LT * 128
    XP = cfx.shape[1]
    FROWS = XP * 8
    me_grp = lax.axis_index("grp")
    me_gx = lax.axis_index("gx")
    me_yz = lax.axis_index("yz")
    full_g = WG == n_gx
    full_h = WH == n_yz
    gs = me_gx if full_g else RG
    hs = me_yz if full_h else RH
    g_start = 0 if full_g else me_gx - RG
    h_start = 0 if full_h else me_yz - RH

    win[...] = jnp.zeros(win.shape, F32)
    planes[...] = jnp.zeros(planes.shape, F32)
    cfx[...] = jnp.zeros(cfx.shape, F32)

    me_of = {"grp": me_grp, "gx": me_gx, "yz": me_yz}
    n_of = {"grp": n_grp, "gx": n_gx, "yz": n_yz}

    def exists(axis, k):
        at = me_of[axis] + k
        return jnp.logical_and(at >= 0, at < n_of[axis])

    peers = [("grp", k) for k in offsets(min(1, n_grp - 1))]
    peers += [("gx", k) for k in offsets(RG)]
    peers += [("yz", k) for k in offsets(RH)]

    barrier = pltpu.get_barrier_semaphore()
    count = jnp.int32(0)
    for axis, k in peers:
        here = exists(axis, k)
        count = count + here.astype(jnp.int32)

        @pl.when(here)
        def _(axis=axis, k=k):
            pl.semaphore_signal(barrier, inc=1, device_id={axis: me_of[axis] + k}, device_id_type=MESH)

    basis = basis_ref[...]
    lane = iota((8, NODES), 1)
    sub = iota((8, NODES), 0)
    v1 = (lane // 64 == sub).astype(F32)
    v2 = ((lane // 8) % 8 == sub).astype(F32)
    v3 = (lane % 8 == sub).astype(F32)

    def build(hi_ref, lo_ref, dims):
        t1 = dot(basis, v1, dims)
        t2 = dot(basis, v2, dims)
        t3 = dot(basis, v3, dims)
        pairs = jnp.concatenate([t2[j : j + 1, :] * t3 for j in range(8)], axis=0)
        for i in range(8):
            hi, lo = split(t1[i : i + 1, :] * pairs)
            hi_ref[i * 64 : (i + 1) * 64, :] = hi
            lo_ref[i * 64 : (i + 1) * 64, :] = lo

    build(e_hi, e_lo, ((1,), (0,)))
    build(t_hi, t_lo, ((0,), (0,)))
    spectrum = dot(eig_ref[...], v1 + v2 + v3)

    node_at = (lane // 64, (lane // 8) % 8, lane % 8)
    side_at = (sub // 4, (sub // 2) % 2, sub % 2)
    restrict = jnp.ones((8, NODES), F32)
    for d in range(3):
        restrict = restrict * jnp.where(side_at[d] == 0, pick(node_at[d], L0), pick(node_at[d], L1))
    on_face = [
        jnp.where(node_at[d] == 7 * side_at[d], restrict, 0.0) for d in range(3)
    ]
    faces = jnp.concatenate(on_face, axis=0)

    YZ = LY * LZ
    NE = LX * YZ
    for x in range(LX):
        for y in range(LY):
            at = x * YZ + y * LZ
            rhs_s[at : at + LZ, :] = rhs_ref[x, y]
    rhs = rhs_s[...]
    row = iota((NE, 1), 0)
    row_x, row_y, row_z = row // YZ, (row // LZ) % LY, row % LZ
    ysel = (iota((YZ, LY), 0) // LZ == iota((YZ, LY), 1)).astype(F32)
    zsel = iota((YZ, LZ), 0) % LZ == iota((YZ, LZ), 1)

    def column(ref):
        parts = []
        for x in range(LX):
            spread = dot(ysel, ref[x].astype(F32))
            parts.append(jnp.sum(jnp.where(zsel, spread, 0.0), axis=1, keepdims=True))
        return parts

    coeff_cols = column(coeff_ref)
    flag_cols = column(flags_ref)
    coeff_col = jnp.concatenate(coeff_cols, axis=0)
    flag_col = jnp.concatenate(flag_cols, axis=0)
    inverse = 1.0 / (coeff_col * spectrum)

    r16 = iota((YZ, 128), 0)
    l16 = iota((YZ, 128), 1)
    spot = (r16 // LZ) * 8 + me_grp * LZ + r16 % LZ
    tail = (l16 == 96 + spot).astype(F32)
    re = iota((NE, 128), 0)
    place = (
        iota((NE, 128), 1) == (re // YZ) * 32 + ((re // LZ) % LY) * 8 + me_grp * LZ + re % LZ
    ).astype(F32)

    b_own = dot(dot(restrict, rhs, ((1,), (1,))), place)
    row8 = iota((8, 128), 0)
    for x in range(LX):
        c_line = jnp.sum(coeff_cols[x] * tail, axis=0, keepdims=True)
        f_line = jnp.sum(flag_cols[x] * tail, axis=0, keepdims=True)
        b_own = b_own + jnp.where(row8 == x, c_line, 0.0) + jnp.where(row8 == LX + x, f_line, 0.0)
    s = dot3(dot3(rhs, e_hi[...], e_lo[...]) * inverse, t_hi[...], t_lo[...])
    s_ref[...] = s
    mine[0:8, :] = b_own
    mine[8:32, :] = dot(dot(faces, s, ((1,), (1,))), place)

    for side in range(2):
        yy, zz = (0, 0) if side == 0 else (LY - 1, LZ - 1)
        for x in range(LX):
            ysend[side, x * LZ : (x + 1) * LZ, :] = s_ref[x * YZ + yy * LZ : x * YZ + (yy + 1) * LZ, :]
            for y in range(LY):
                at = x * YZ + y * LZ + zz
                zsend[side, x * LY + y : x * LY + y + 1, :] = s_ref[at : at + 1, :]

    def face_copies():
        found = []
        for n, (axis, k) in enumerate(
            [("gx", -1), ("gx", 1), ("yz", -1), ("yz", 1), ("grp", -1), ("grp", 1)]
        ):
            if n_of[axis] == 1:
                continue
            side = 0 if k < 0 else 1
            if axis == "gx":
                at = 0 if side == 0 else (LX - 1) * YZ
                src, dst = s_ref.at[pl.ds(at, YZ)], xrecv.at[1 - side]
            elif axis == "yz":
                src, dst = ysend.at[side], yrecv.at[1 - side]
            else:
                src, dst = zsend.at[side], zrecv.at[1 - side]
            copy = pltpu.make_async_remote_copy(
                src_ref=src, dst_ref=dst, send_sem=fsend.at[n], recv_sem=frecv.at[n],
                device_id={axis: me_of[axis] + k}, device_id_type=MESH,
            )
            found.append((axis, k, copy))
        return found

    def phase_copies(axis):
        found = []
        for axis_p, k in peers:
            n = peers.index((axis_p, k))
            if axis_p != axis:
                continue
            if axis == "grp":
                src, dst = mine, other
            elif axis == "gx":
                src, dst = win.at[hs, gs], win.at[hs, gs if full_g else RG - k]
                if abs(k) > RGF:
                    src, dst = src.at[pl.ds(0, 8)], dst.at[pl.ds(0, 8)]
            else:
                src, dst = win.at[hs], win.at[hs if full_h else RH - k]
                if abs(k) > RHF:
                    src, dst = src.at[:, pl.ds(0, 8)], dst.at[:, pl.ds(0, 8)]
            copy = pltpu.make_async_remote_copy(
                src_ref=src, dst_ref=dst, send_sem=send_sem.at[n], recv_sem=recv_sem.at[n],
                device_id={axis: me_of[axis] + k}, device_id_type=MESH,
            )
            found.append((axis, k, copy))
        return found

    def recv_of(axis, k, copy_list):
        return next(c for a, j, c in copy_list if (a, j) == (axis, k))

    def start_all(copies):
        for axis, k, copy in copies:
            @pl.when(exists(axis, k))
            def _(copy=copy):
                copy.start()

    def wait_recv(copies):
        for axis, k, copy in copies:
            @pl.when(exists(axis, -k))
            def _(copy=copy):
                copy.wait_recv()

    def wait_send(copies):
        for axis, k, copy in copies:
            @pl.when(exists(axis, k))
            def _(copy=copy):
                copy.wait_send()

    pl.semaphore_wait(barrier, count)

    grp_copies = phase_copies("grp")
    gx_copies = phase_copies("gx")
    yz_copies = phase_copies("yz")
    next_door = face_copies()
    start_all(grp_copies)
    wait_recv(grp_copies)
    if n_grp > 1:
        win[hs, gs] = mine[...] + other[...]
    else:
        win[hs, gs] = mine[...]
    start_all(gx_copies)
    start_all(next_door)
    wait_recv(gx_copies)
    start_all(yz_copies)
    wait_recv(next_door)

    own_at = (me_gx * LX + row_x, me_yz * LY + row_y, me_grp * LZ + row_z)
    totals = (n_gx * LX, n_yz * LY, n_grp * LZ)
    node_lane = iota((1, NODES), 1)
    node_of = (node_lane // 64, (node_lane // 8) % 8, node_lane % 8)
    strides = (64, 8, 1)
    face_s = jnp.zeros((NE, NODES), F32)
    for d in range(3):
        for side in range(2):
            if d == 0:
                if side == 0:
                    beside = jnp.concatenate([xrecv[0], s[: NE - YZ]], axis=0)
                else:
                    beside = jnp.concatenate([s[YZ:], xrecv[1]], axis=0)
            else:
                step = LZ if d == 1 else 1
                nb[...] = pltpu.roll(s, step if side == 0 else NE - step, 0)
                for x in range(LX):
                    if d == 1:
                        at = x * YZ + (0 if side == 0 else (LY - 1) * LZ)
                        nb[at : at + LZ, :] = yrecv[side, x * LZ : (x + 1) * LZ, :]
                    else:
                        for y in range(LY):
                            at = x * YZ + y * LZ + (0 if side == 0 else LZ - 1)
                            nb[at : at + 1, :] = zrecv[side, x * LY + y : x * LY + y + 1, :]
                beside = nb[...]
            has = own_at[d] > 0 if side == 0 else own_at[d] < totals[d] - 1
            gain = jnp.where(has, 1.0, flag_col)
            shift = 7 * strides[d]
            moved = pltpu.roll(beside, NODES - shift if side == 0 else shift, 1)
            term = gain * s - jnp.where(has, moved, 0.0)
            face_s = face_s + jnp.where(node_of[d] == 7 * side, term, 0.0)

    wait_recv(yz_copies)

    lane_slot = iota((32, L), 1) // 32
    for g in range(WG):
        cf_plane = jnp.zeros((8, L), F32)
        tiles = []
        for h in range(WH):
            tile = win[h, g]
            if L > 128:
                tile = jnp.concatenate([tile, jnp.zeros((32, L - 128), F32)], axis=1)
            tiles.append(tile)
            moved = pltpu.roll(tile[0:8], (32 * (h - 3)) % L, 1)
            cf_plane = jnp.where(lane_slot[0:8] == h, moved, cf_plane)
        for x in range(LX):
            plane = jnp.zeros((32, L), F32)
            for h in range(WH):
                amount = (32 * (h - x)) % L
                moved = pltpu.roll(tiles[h], amount, 1) if amount else tiles[h]
                plane = jnp.where(lane_slot == h, moved, plane)
            at = (g * LX + x) * 8
            for f in range(4):
                for t in range(LT):
                    part = plane[f * 8 : f * 8 + 8, t * 128 : (t + 1) * 128]
                    planes[t, f * FROWS + at : f * FROWS + at + 8, :] = part
        cfx[0, g * LX : (g + 1) * LX, :] = cf_plane[0:LX]
        cfx[1, g * LX : (g + 1) * LX, :] = cf_plane[LX : 2 * LX]

    def strided(ref, start, stride):
        parts = [ref[t, pl.ds(start, XP, stride=stride), :] for t in range(LT)]
        return parts[0] if LT == 1 else jnp.concatenate(parts, axis=1)

    def store_strided(ref, start, stride, value):
        for t in range(LT):
            ref[t, pl.ds(start, XP, stride=stride), :] = value[:, t * 128 : (t + 1) * 128]

    def field(f):
        return [strided(planes, f * FROWS + a, 8) for a in range(8)]

    rhs1 = field(0)
    proj = [field(1 + d) for d in range(3)]
    coeff = cfx[0]
    flag = cfx[1]
    pos = (
        g_start * LX + iota((XP, L), 0),
        h_start * LY + iota((XP, L), 1) // 8,
        iota((XP, L), 1) % 8,
    )
    has = [(pos[d] > 0, pos[d] < totals[d] - 1) for d in range(3)]
    gain = [[jnp.where(has[d][q], 1.0, flag) for q in range(2)] for d in range(3)]
    roll_axis = (0, 1, 1)
    roll_step = (1, 8, 1)
    bit = (4, 2, 1)

    def side_of(a, d):
        return (a // bit[d]) % 2

    def beside_of(v, a, d):
        q = side_of(a, d)
        size = XP if d == 0 else L
        step = roll_step[d] if q == 0 else size - roll_step[d]
        return jnp.where(has[d][q], pltpu.roll(v[a ^ bit[d]], step, roll_axis[d]), 0.0)

    def jump(v, a, d):
        return gain[d][side_of(a, d)] * v[a] - beside_of(v, a, d)

    diag = [
        coeff * 3.5 + gain[0][side_of(a, 0)] + gain[1][side_of(a, 1)] + gain[2][side_of(a, 2)]
        for a in range(8)
    ]

    def coarse_apply(v):
        out = []
        for a in range(8):
            flips = v[a ^ 4] + v[a ^ 2] + v[a ^ 1]
            sides = beside_of(v, a, 0) + beside_of(v, a, 1) + beside_of(v, a, 2)
            out.append(diag[a] * v[a] - coeff * flips - sides)
        return out

    center = 0.5 * (CHEB_HIGH + CHEB_LOW)
    half_width = 0.5 * (CHEB_HIGH - CHEB_LOW)
    inverse_diag = 1.0 / (coeff * 3.5 + 3.0)

    def cheb(f):
        sigma = center / half_width
        rho = 1.0 / sigma
        remain = f
        first = inverse_diag * (1.0 / center)
        update = [first * r for r in remain]
        result = update
        for _ in range(CHEB - 1):
            applied = coarse_apply(update)
            remain = [r - t for r, t in zip(remain, applied)]
            rho_next = 1.0 / (2.0 * sigma - rho)
            weight = inverse_diag * (2.0 * rho_next / half_width)
            update = [(rho_next * rho) * u + weight * r for u, r in zip(update, remain)]
            result = [t + u for t, u in zip(result, update)]
            rho = rho_next
        return result

    col = iota((8, 8), 0)
    w = [jnp.sum(pick(col, t) * basis, axis=0, keepdims=True) for t in (L0, L1)]
    eig = eig_ref[...]
    stiff = [[jnp.sum(eig * w[p] * w[q], axis=1, keepdims=True) for q in range(2)] for p in range(2)]

    def mass(v, d):
        return [MASS_SAME * v[a] + MASS_OTHER * v[a ^ bit[d]] for a in range(8)]

    c1 = cheb(rhs1)
    m3 = mass(c1, 2)
    m23 = mass(m3, 1)
    m13 = mass(m3, 0)
    m12 = mass(mass(c1, 1), 0)
    masses = (m23, m13, m12)
    rhs2 = []
    for a in range(8):
        inner = 0.0
        for d in range(3):
            q = side_of(a, d)
            inner = inner + stiff[q][q] * masses[d][a] + stiff[q][1 - q] * masses[d][a ^ bit[d]]
        rhs2.append(0.5 * rhs1[a] - 0.5 * coeff * inner)
    for d in range(3):
        both = [proj[d][a] + masses[d][a] for a in range(8)]
        rhs2 = [rhs2[a] - jump(both, a, d) for a in range(8)]

    first_row = gs * LX
    absolute = hs * 32 + (iota((YZ, L), 0) // LZ) * 8 + me_grp * LZ + iota((YZ, L), 0) % LZ
    take = (iota((YZ, L), 1) == absolute).astype(F32)

    def own_values(ref, comps):
        parts = []
        for x in range(LX):
            start = pl.multiple_of((first_row + x) * comps, 8)
            part = 0.0
            for t in range(LT):
                lanes = take[:, t * 128 : (t + 1) * 128]
                part = part + dot(lanes, ref[t, pl.ds(start, comps), :], ((1,), (1,)))
            parts.append(part)
        return jnp.concatenate(parts, axis=0)

    for d in range(3):
        for a in range(8):
            store_strided(ext3, d * 8 + a, 24, jump(c1, a, d))
    face_c = dot(own_values(ext3, 24), faces)
    total = face_s + face_c
    smooth2 = dot3(dot3(total, e_hi[...], e_lo[...]) * inverse, t_hi[...], t_lo[...])

    c2 = cheb(rhs2)
    for a in range(8):
        store_strided(ext1, a, 8, 0.25 * c1[a] + 0.5 * c2[a])
    lifted = dot(own_values(ext1, 8), restrict)
    out_ref[...] = 0.75 * s + lifted - 0.5 * smooth2

    for copies in (grp_copies, gx_copies, yz_copies, next_door):
        wait_send(copies)


def body(cfg, rhs, coeff, flags, basis, eigenvalues):
    n_grp, n_gx, n_yz, LX, LY, LZ, WG, WH, RG, RH, RGF, RHF = cfg
    NE = LX * LY * LZ
    L = -(-(WH * 32) // 128) * 128
    XP = -(-(WG * LX) // 8) * 8
    V = pltpu.VMEM
    n_peers = 2 * (1 + RG + RH)
    out = pl.pallas_call(
        functools.partial(kernel, cfg),
        out_shape=jax.ShapeDtypeStruct((NE, NODES), F32),
        in_specs=[pl.BlockSpec(memory_space=V)] * 5,
        out_specs=pl.BlockSpec(memory_space=V),
        scratch_shapes=[
            V((32, 128), F32),
            V((32, 128), F32),
            V((WH, WG, 32, 128), F32),
            V((L // 128, 4 * XP * 8, 128), F32),
            V((2, XP, L), F32),
            V((L // 128, XP * 24, 128), F32),
            V((L // 128, XP * 8, 128), F32),
            V((NE, NODES), F32),
            V((NE, NODES), F32),
            V((NODES, NODES), BF16),
            V((NODES, NODES), BF16),
            V((NODES, NODES), BF16),
            V((NODES, NODES), BF16),
            V((2, 16, NODES), F32),
            V((2, 16, NODES), F32),
            V((2, 16, NODES), F32),
            V((2, 16, NODES), F32),
            V((2, LY * LZ, NODES), F32),
            V((NE, NODES), F32),
            pltpu.SemaphoreType.DMA((n_peers,)),
            pltpu.SemaphoreType.DMA((n_peers,)),
            pltpu.SemaphoreType.DMA((6,)),
            pltpu.SemaphoreType.DMA((6,)),
        ],
        compiler_params=pltpu.CompilerParams(
            collective_id=0, has_side_effects=True, vmem_limit_bytes=32 * 1024 * 1024
        ),
    )(rhs, coeff, flags, basis, eigenvalues.reshape(1, DEG1))
    return out.reshape(rhs.shape)


def solution(mesh):
    n_grp, n_gx, n_yz = (mesh.shape[a] for a in ("grp", "gx", "yz"))

    def call(rhs, coeff, flags, basis, eigenvalues):
        EX, EY, EZ = rhs.shape[:3]
        LX, LY, LZ = EX // n_gx, EY // n_yz, EZ // n_grp
        assert LX <= 3 and LY <= 4 and EZ <= 8 and n_grp <= 2

        def reach(steps, local, count):
            return min(-(-steps // local), count - 1)

        RG, RH = reach(REACH, LX, n_gx), reach(REACH, LY, n_yz)
        RGF, RHF = reach(REACH_FACE, LX, n_gx), reach(REACH_FACE, LY, n_yz)
        WG = n_gx if n_gx <= 2 * RG + 1 else 2 * RG + 1
        WH = n_yz if n_yz <= 2 * RH + 1 else 2 * RH + 1
        cfg = (n_grp, n_gx, n_yz, LX, LY, LZ, WG, WH, RG, RH, RGF, RHF)
        spec = (P("gx", "yz", "grp", None), P("gx", "yz", "grp"), P("gx", "yz", "grp"), P(), P())
        run = jax.shard_map(
            functools.partial(body, cfg), mesh=mesh, in_specs=spec,
            out_specs=P("gx", "yz", "grp", None), check_vma=False,
        )
        return run(rhs, coeff, flags, basis, eigenvalues)

    return call
```

```python
import functools

import jax
import jax.numpy as jnp
import numpy as np
from jax import lax
from jax.experimental import pallas as pl
from jax.experimental.pallas import tpu as pltpu
from jax.sharding import PartitionSpec as P

DEG1 = 8
NODES = 512
CHEB = 4
CHEB_LOW = 0.1
CHEB_HIGH = 2.0
REACH = 7
REACH_FACE = 4
GLL_POINTS = (
    -1.0,
    -0.8717401485096066,
    -0.5917001814331423,
    -0.2092992179024789,
    0.2092992179024789,
    0.5917001814331423,
    0.8717401485096066,
    1.0,
)
L0 = [(1.0 - x) * 0.5 for x in GLL_POINTS]
L1 = [(1.0 + x) * 0.5 for x in GLL_POINTS]
MASS_SAME = sum(a * a for a in L0)
MASS_OTHER = sum(a * b for a, b in zip(L0, L1))
HIGHEST = lax.Precision.HIGHEST
MESH = pl.DeviceIdType.MESH
F32 = jnp.float32
BF16 = jnp.bfloat16


def iota(shape, dim):
    return lax.broadcasted_iota(jnp.int32, shape, dim)


def dot(a, b, dims=((1,), (0,))):
    return lax.dot_general(a, b, (dims, ((), ())), precision=HIGHEST, preferred_element_type=F32)


def split(x):
    hi = x.astype(BF16)
    return hi, (x - hi.astype(F32)).astype(BF16)


def dot3(x, hi, lo):
    xh, xl = split(x)
    d = functools.partial(jnp.dot, preferred_element_type=F32)
    return d(xh, hi) + (d(xl, hi) + d(xh, lo))


def pick(index, table):
    out = jnp.full(index.shape, table[0], F32)
    for i in range(1, len(table)):
        out = jnp.where(index == i, table[i], out)
    return out


def kernel(
    cfg,
    rhs_hbm, coeff_hbm, flags_hbm, basis_hbm, eig_hbm,
    out_ref,
    rhs_ref, coeff_ref, flags_ref, basis_ref, eig_ref,
    mine_b, other_b, mine_p, other_p, win_b, win_p, planes, cfx, ext3, ext1,
    rhs_s, s_ref, e_hi, e_lo, t_hi, t_lo,
    ysend, yrecv, zsend, zrecv, xrecv, nb,
    in_sem, b_send, b_recv, p_send, p_recv, g_send, g_recv, fsend, frecv,
):
    n_grp, n_gx, n_yz, LX, LY, LZ, WG, WH, RG, RH = cfg
    LT = planes.shape[0]
    L = LT * 128
    XP = cfx.shape[1]
    FROWS = XP * 8
    me_grp = lax.axis_index("grp")
    me_gx = lax.axis_index("gx")
    me_yz = lax.axis_index("yz")
    full_g = WG == n_gx
    full_h = WH == n_yz
    gs = me_gx if full_g else RG
    hs = me_yz if full_h else RH
    g_start = 0 if full_g else me_gx - RG
    h_start = 0 if full_h else me_yz - RH

    loads = []
    pairs_in = [
        (basis_hbm, basis_ref), (eig_hbm, eig_ref), (rhs_hbm, rhs_ref),
        (coeff_hbm, coeff_ref), (flags_hbm, flags_ref),
    ]
    for n, (src, dst) in enumerate(pairs_in):
        load = pltpu.make_async_copy(src, dst, in_sem.at[n])
        load.start()
        loads.append(load)
    win_b[...] = jnp.zeros(win_b.shape, F32)
    win_p[...] = jnp.zeros(win_p.shape, F32)

    me_of = {"grp": me_grp, "gx": me_gx, "yz": me_yz}
    n_of = {"grp": n_grp, "gx": n_gx, "yz": n_yz}

    def exists(axis, k):
        at = me_of[axis] + k
        return jnp.logical_and(at >= 0, at < n_of[axis])

    def cost(k, local):
        return 0 if k == 0 else (abs(k) - 1) * local + 1

    def around(reach):
        return [
            (kg, kh)
            for kg in range(-RG, RG + 1)
            for kh in range(-RH, RH + 1)
            if (kg, kh) != (0, 0) and cost(kg, LX) + cost(kh, LY) <= reach
        ]

    def target(key):
        return {axis: me_of[axis] + k for axis, k in key if k}

    def present(key):
        there = None
        for axis, k in key:
            if k:
                here = exists(axis, k)
                there = here if there is None else jnp.logical_and(there, here)
        return there

    grp_keys = [(("grp", k),) for k in (-1, 1)] if n_grp > 1 else []
    b_keys = [(("gx", kg), ("yz", kh)) for kg, kh in around(REACH)]
    p_keys = [(("gx", kg), ("yz", kh)) for kg, kh in around(REACH_FACE)]

    barrier = pltpu.get_barrier_semaphore()
    count = jnp.int32(0)
    for key in grp_keys + b_keys:
        here = present(key)
        count = count + here.astype(jnp.int32)

        @pl.when(here)
        def _(key=key):
            pl.semaphore_signal(barrier, inc=1, device_id=target(key), device_id_type=MESH)

    lane = iota((8, NODES), 1)
    sub = iota((8, NODES), 0)
    v1 = (lane // 64 == sub).astype(F32)
    v2 = ((lane // 8) % 8 == sub).astype(F32)
    v3 = (lane % 8 == sub).astype(F32)

    node_at = (lane // 64, (lane // 8) % 8, lane % 8)
    side_at = (sub // 4, (sub // 2) % 2, sub % 2)
    restrict = jnp.ones((8, NODES), F32)
    for d in range(3):
        restrict = restrict * jnp.where(side_at[d] == 0, pick(node_at[d], L0), pick(node_at[d], L1))
    on_face = [
        jnp.where(node_at[d] == 7 * side_at[d], restrict, 0.0) for d in range(3)
    ]
    faces = jnp.concatenate(on_face, axis=0)

    YZ = LY * LZ
    NE = LX * YZ
    row = iota((NE, 1), 0)
    row_x, row_y, row_z = row // YZ, (row // LZ) % LY, row % LZ
    ysel = (iota((YZ, LY), 0) // LZ == iota((YZ, LY), 1)).astype(F32)
    zsel = iota((YZ, LZ), 0) % LZ == iota((YZ, LZ), 1)

    r16 = iota((YZ, 128), 0)
    l16 = iota((YZ, 128), 1)
    spot = (r16 // LZ) * 8 + me_grp * LZ + r16 % LZ
    tail = (l16 == 96 + spot).astype(F32)
    re = iota((NE, 128), 0)
    place = (
        iota((NE, 128), 1) == (re // YZ) * 32 + ((re // LZ) % LY) * 8 + me_grp * LZ + re % LZ
    ).astype(F32)

    loads[0].wait()
    loads[1].wait()
    basis = basis_ref[...]

    def build(hi_ref, lo_ref, dims):
        t1 = dot(basis, v1, dims)
        t2 = dot(basis, v2, dims)
        t3 = dot(basis, v3, dims)
        pairs = jnp.concatenate([t2[j : j + 1, :] * t3 for j in range(8)], axis=0)
        for i in range(8):
            hi, lo = split(t1[i : i + 1, :] * pairs)
            hi_ref[i * 64 : (i + 1) * 64, :] = hi
            lo_ref[i * 64 : (i + 1) * 64, :] = lo

    build(e_hi, e_lo, ((1,), (0,)))
    build(t_hi, t_lo, ((0,), (0,)))
    spectrum = dot(eig_ref[...], v1 + v2 + v3)

    for load in loads[2:]:
        load.wait()
    for x in range(LX):
        for y in range(LY):
            at = x * YZ + y * LZ
            rhs_s[at : at + LZ, :] = rhs_ref[x, y]
    rhs = rhs_s[...]
    def column(ref):
        parts = []
        for x in range(LX):
            spread = dot(ysel, ref[x].astype(F32))
            parts.append(jnp.sum(jnp.where(zsel, spread, 0.0), axis=1, keepdims=True))
        return parts

    coeff_cols = column(coeff_ref)
    flag_cols = column(flags_ref)
    coeff_col = jnp.concatenate(coeff_cols, axis=0)
    flag_col = jnp.concatenate(flag_cols, axis=0)
    inverse = 1.0 / (coeff_col * spectrum)

    b_own = dot(dot(restrict, rhs, ((1,), (1,))), place)
    row8 = iota((8, 128), 0)
    for x in range(LX):
        c_line = jnp.sum(coeff_cols[x] * tail, axis=0, keepdims=True)
        f_line = jnp.sum(flag_cols[x] * tail, axis=0, keepdims=True)
        b_own = b_own + jnp.where(row8 == x, c_line, 0.0) + jnp.where(row8 == LX + x, f_line, 0.0)
    mine_b[...] = b_own

    def remote(src, dst, send, recv, n, key):
        copy = pltpu.make_async_remote_copy(
            src_ref=src, dst_ref=dst, send_sem=send.at[n], recv_sem=recv.at[n],
            device_id=target(key), device_id_type=MESH,
        )
        return key, copy

    def around_copies(ref, keys, send, recv):
        found = []
        for n, key in enumerate(keys):
            kg, kh = key[0][1], key[1][1]
            slot = (hs if full_h else RH - kh, gs if full_g else RG - kg)
            found.append(remote(ref.at[hs, gs], ref.at[slot[0], slot[1]], send, recv, n, key))
        return found

    def start_all(copies):
        for key, copy in copies:
            @pl.when(present(key))
            def _(copy=copy):
                copy.start()

    def wait_recv(copies):
        for key, copy in copies:
            @pl.when(present([(axis, -k) for axis, k in key]))
            def _(copy=copy):
                copy.wait_recv()

    def wait_send(copies):
        for key, copy in copies:
            @pl.when(present(key))
            def _(copy=copy):
                copy.wait_send()

    grp_b = [remote(mine_b, other_b, g_send, g_recv, n, key) for n, key in enumerate(grp_keys)]
    grp_p = [remote(mine_p, other_p, g_send, g_recv, 2 + n, key) for n, key in enumerate(grp_keys)]
    all_b = around_copies(win_b, b_keys, b_send, b_recv)
    all_p = around_copies(win_p, p_keys, p_send, p_recv)

    pl.semaphore_wait(barrier, count)
    start_all(grp_b)
    s = dot3(dot3(rhs, e_hi[...], e_lo[...]) * inverse, t_hi[...], t_lo[...])
    s_ref[...] = s
    wait_recv(grp_b)
    win_b[hs, gs] = mine_b[...] + other_b[...] if n_grp > 1 else mine_b[...]
    start_all(all_b)
    mine_p[...] = dot(dot(faces, s, ((1,), (1,))), place)
    start_all(grp_p)

    for side in range(2):
        yy, zz = (0, 0) if side == 0 else (LY - 1, LZ - 1)
        for x in range(LX):
            ysend[side, x * LZ : (x + 1) * LZ, :] = s_ref[x * YZ + yy * LZ : x * YZ + (yy + 1) * LZ, :]
            for y in range(LY):
                at = x * YZ + y * LZ + zz
                zsend[side, x * LY + y : x * LY + y + 1, :] = s_ref[at : at + 1, :]

    def face_copies():
        found = []
        for n, (axis, k) in enumerate(
            [("gx", -1), ("gx", 1), ("yz", -1), ("yz", 1), ("grp", -1), ("grp", 1)]
        ):
            if n_of[axis] == 1:
                continue
            side = 0 if k < 0 else 1
            if axis == "gx":
                at = 0 if side == 0 else (LX - 1) * YZ
                src, dst = s_ref.at[pl.ds(at, YZ)], xrecv.at[1 - side]
            elif axis == "yz":
                src, dst = ysend.at[side], yrecv.at[1 - side]
            else:
                src, dst = zsend.at[side], zrecv.at[1 - side]
            found.append(remote(src, dst, fsend, frecv, n, ((axis, k),)))
        return found

    next_door = face_copies()
    start_all(next_door)
    wait_recv(grp_p)
    win_p[hs, gs] = mine_p[...] + other_p[...] if n_grp > 1 else mine_p[...]
    start_all(all_p)
    planes[...] = jnp.zeros(planes.shape, F32)
    cfx[...] = jnp.zeros(cfx.shape, F32)
    wait_recv(next_door)

    own_at = (me_gx * LX + row_x, me_yz * LY + row_y, me_grp * LZ + row_z)
    totals = (n_gx * LX, n_yz * LY, n_grp * LZ)
    node_lane = iota((1, NODES), 1)
    node_of = (node_lane // 64, (node_lane // 8) % 8, node_lane % 8)
    strides = (64, 8, 1)
    face_s = jnp.zeros((NE, NODES), F32)
    for d in range(3):
        for side in range(2):
            if d == 0:
                if side == 0:
                    beside = jnp.concatenate([xrecv[0], s[: NE - YZ]], axis=0)
                else:
                    beside = jnp.concatenate([s[YZ:], xrecv[1]], axis=0)
            else:
                step = LZ if d == 1 else 1
                nb[...] = pltpu.roll(s, step if side == 0 else NE - step, 0)
                for x in range(LX):
                    if d == 1:
                        at = x * YZ + (0 if side == 0 else (LY - 1) * LZ)
                        nb[at : at + LZ, :] = yrecv[side, x * LZ : (x + 1) * LZ, :]
                    else:
                        for y in range(LY):
                            at = x * YZ + y * LZ + (0 if side == 0 else LZ - 1)
                            nb[at : at + 1, :] = zrecv[side, x * LY + y : x * LY + y + 1, :]
                beside = nb[...]
            has = own_at[d] > 0 if side == 0 else own_at[d] < totals[d] - 1
            gain = jnp.where(has, 1.0, flag_col)
            shift = 7 * strides[d]
            moved = pltpu.roll(beside, NODES - shift if side == 0 else shift, 1)
            term = gain * s - jnp.where(has, moved, 0.0)
            face_s = face_s + jnp.where(node_of[d] == 7 * side, term, 0.0)

    wait_recv(all_b)

    def spread(win, rows, first_field):
        lane_slot = iota((rows, L), 1) // 32
        for g in range(WG):
            cf_plane = jnp.zeros((rows, L), F32)
            tiles = []
            for h in range(WH):
                tile = win[h, g]
                if L > 128:
                    tile = jnp.concatenate([tile, jnp.zeros((rows, L - 128), F32)], axis=1)
                tiles.append(tile)
                if first_field == 0:
                    moved = pltpu.roll(tile, (32 * (h - 3)) % L, 1)
                    cf_plane = jnp.where(lane_slot == h, moved, cf_plane)
            for x in range(LX):
                plane = jnp.zeros((rows, L), F32)
                for h in range(WH):
                    amount = (32 * (h - x)) % L
                    moved = pltpu.roll(tiles[h], amount, 1) if amount else tiles[h]
                    plane = jnp.where(lane_slot == h, moved, plane)
                at = (g * LX + x) * 8
                for f in range(rows // 8):
                    to = (first_field + f) * FROWS + at
                    for t in range(LT):
                        part = plane[f * 8 : f * 8 + 8, t * 128 : (t + 1) * 128]
                        planes[t, to : to + 8, :] = part
            if first_field == 0:
                cfx[0, g * LX : (g + 1) * LX, :] = cf_plane[0:LX]
                cfx[1, g * LX : (g + 1) * LX, :] = cf_plane[LX : 2 * LX]

    spread(win_b, 8, 0)

    def strided(ref, start, stride):
        parts = [ref[t, pl.ds(start, XP, stride=stride), :] for t in range(LT)]
        return parts[0] if LT == 1 else jnp.concatenate(parts, axis=1)

    def store_strided(ref, start, stride, value):
        for t in range(LT):
            ref[t, pl.ds(start, XP, stride=stride), :] = value[:, t * 128 : (t + 1) * 128]

    def field(f):
        return [strided(planes, f * FROWS + a, 8) for a in range(8)]

    rhs1 = field(0)
    coeff = cfx[0]
    flag = cfx[1]
    pos = (
        g_start * LX + iota((XP, L), 0),
        h_start * LY + iota((XP, L), 1) // 8,
        iota((XP, L), 1) % 8,
    )
    has = [(pos[d] > 0, pos[d] < totals[d] - 1) for d in range(3)]
    gain = [[jnp.where(has[d][q], 1.0, flag) for q in range(2)] for d in range(3)]
    roll_axis = (0, 1, 1)
    roll_step = (1, 8, 1)
    bit = (4, 2, 1)

    def side_of(a, d):
        return (a // bit[d]) % 2

    def beside_of(v, a, d):
        q = side_of(a, d)
        size = XP if d == 0 else L
        step = roll_step[d] if q == 0 else size - roll_step[d]
        return jnp.where(has[d][q], pltpu.roll(v[a ^ bit[d]], step, roll_axis[d]), 0.0)

    def jump(v, a, d):
        return gain[d][side_of(a, d)] * v[a] - beside_of(v, a, d)

    diag = [
        coeff * 3.5 + gain[0][side_of(a, 0)] + gain[1][side_of(a, 1)] + gain[2][side_of(a, 2)]
        for a in range(8)
    ]

    def coarse_apply(v):
        out = []
        for a in range(8):
            flips = v[a ^ 4] + v[a ^ 2] + v[a ^ 1]
            sides = beside_of(v, a, 0) + beside_of(v, a, 1) + beside_of(v, a, 2)
            out.append(diag[a] * v[a] - coeff * flips - sides)
        return out

    center = 0.5 * (CHEB_HIGH + CHEB_LOW)
    half_width = 0.5 * (CHEB_HIGH - CHEB_LOW)
    inverse_diag = 1.0 / (coeff * 3.5 + 3.0)

    def cheb(f):
        sigma = center / half_width
        rho = 1.0 / sigma
        remain = f
        first = inverse_diag * (1.0 / center)
        update = [first * r for r in remain]
        result = update
        for _ in range(CHEB - 1):
            applied = coarse_apply(update)
            remain = [r - t for r, t in zip(remain, applied)]
            rho_next = 1.0 / (2.0 * sigma - rho)
            weight = inverse_diag * (2.0 * rho_next / half_width)
            update = [(rho_next * rho) * u + weight * r for u, r in zip(update, remain)]
            result = [t + u for t, u in zip(result, update)]
            rho = rho_next
        return result

    col = iota((8, 8), 0)
    w = [jnp.sum(pick(col, t) * basis, axis=0, keepdims=True) for t in (L0, L1)]
    eig = eig_ref[...]
    stiff = [[jnp.sum(eig * w[p] * w[q], axis=1, keepdims=True) for q in range(2)] for p in range(2)]

    def mass(v, d):
        return [MASS_SAME * v[a] + MASS_OTHER * v[a ^ bit[d]] for a in range(8)]

    c1 = cheb(rhs1)
    m3 = mass(c1, 2)
    m23 = mass(m3, 1)
    m13 = mass(m3, 0)
    m12 = mass(mass(c1, 1), 0)
    masses = (m23, m13, m12)
    rhs2 = []
    for a in range(8):
        inner = 0.0
        for d in range(3):
            q = side_of(a, d)
            inner = inner + stiff[q][q] * masses[d][a] + stiff[q][1 - q] * masses[d][a ^ bit[d]]
        rhs2.append(0.5 * rhs1[a] - 0.5 * coeff * inner)
    first_row = gs * LX
    absolute = hs * 32 + (iota((YZ, L), 0) // LZ) * 8 + me_grp * LZ + iota((YZ, L), 0) % LZ
    take = (iota((YZ, L), 1) == absolute).astype(F32)

    def own_values(ref, comps):
        parts = []
        for x in range(LX):
            start = pl.multiple_of((first_row + x) * comps, 8)
            part = 0.0
            for t in range(LT):
                lanes = take[:, t * 128 : (t + 1) * 128]
                part = part + dot(lanes, ref[t, pl.ds(start, comps), :], ((1,), (1,)))
            parts.append(part)
        return jnp.concatenate(parts, axis=0)

    for d in range(3):
        for a in range(8):
            store_strided(ext3, d * 8 + a, 24, jump(c1, a, d))
    face_c = dot(own_values(ext3, 24), faces)
    total = face_s + face_c
    smooth2 = dot3(dot3(total, e_hi[...], e_lo[...]) * inverse, t_hi[...], t_lo[...])

    wait_recv(all_p)
    spread(win_p, 24, 1)
    proj = [field(1 + d) for d in range(3)]
    for d in range(3):
        both = [proj[d][a] + masses[d][a] for a in range(8)]
        rhs2 = [rhs2[a] - jump(both, a, d) for a in range(8)]
    c2 = cheb(rhs2)
    for a in range(8):
        store_strided(ext1, a, 8, 0.25 * c1[a] + 0.5 * c2[a])
    lifted = dot(own_values(ext1, 8), restrict)
    out_ref[...] = 0.75 * s + lifted - 0.5 * smooth2

    for copies in (grp_b, grp_p, all_b, all_p, next_door):
        wait_send(copies)


def body(cfg, rhs, coeff, flags, basis, eigenvalues):
    n_grp, n_gx, n_yz, LX, LY, LZ, WG, WH, RG, RH = cfg
    NE = LX * LY * LZ
    L = -(-(WH * 32) // 128) * 128
    XP = -(-(WG * LX) // 8) * 8
    V = pltpu.VMEM
    n_peers = (2 * RG + 1) * (2 * RH + 1)
    out = pl.pallas_call(
        functools.partial(kernel, cfg),
        out_shape=jax.ShapeDtypeStruct((NE, NODES), F32),
        in_specs=[pl.BlockSpec(memory_space=pltpu.HBM)] * 5,
        out_specs=pl.BlockSpec(memory_space=V),
        scratch_shapes=[
            V(rhs.shape, F32),
            V(coeff.shape, F32),
            V(flags.shape, jnp.int32),
            V(basis.shape, F32),
            V((1, DEG1), F32),
            V((8, 128), F32),
            V((8, 128), F32),
            V((24, 128), F32),
            V((24, 128), F32),
            V((WH, WG, 8, 128), F32),
            V((WH, WG, 24, 128), F32),
            V((L // 128, 4 * XP * 8, 128), F32),
            V((2, XP, L), F32),
            V((L // 128, XP * 24, 128), F32),
            V((L // 128, XP * 8, 128), F32),
            V((NE, NODES), F32),
            V((NE, NODES), F32),
            V((NODES, NODES), BF16),
            V((NODES, NODES), BF16),
            V((NODES, NODES), BF16),
            V((NODES, NODES), BF16),
            V((2, 16, NODES), F32),
            V((2, 16, NODES), F32),
            V((2, 16, NODES), F32),
            V((2, 16, NODES), F32),
            V((2, LY * LZ, NODES), F32),
            V((NE, NODES), F32),
            pltpu.SemaphoreType.DMA((5,)),
            pltpu.SemaphoreType.DMA((n_peers,)),
            pltpu.SemaphoreType.DMA((n_peers,)),
            pltpu.SemaphoreType.DMA((n_peers,)),
            pltpu.SemaphoreType.DMA((n_peers,)),
            pltpu.SemaphoreType.DMA((4,)),
            pltpu.SemaphoreType.DMA((4,)),
            pltpu.SemaphoreType.DMA((6,)),
            pltpu.SemaphoreType.DMA((6,)),
        ],
        compiler_params=pltpu.CompilerParams(
            collective_id=0, has_side_effects=True, vmem_limit_bytes=60 * 1024 * 1024
        ),
    )(rhs, coeff, flags, basis, eigenvalues.reshape(1, DEG1))
    return out.reshape(rhs.shape)


def solution(mesh):
    n_grp, n_gx, n_yz = (mesh.shape[a] for a in ("grp", "gx", "yz"))

    def call(rhs, coeff, flags, basis, eigenvalues):
        EX, EY, EZ = rhs.shape[:3]
        LX, LY, LZ = EX // n_gx, EY // n_yz, EZ // n_grp
        assert LX <= 3 and LY <= 4 and EZ <= 8 and n_grp <= 2

        def reach(steps, local, count):
            return min(-(-steps // local), count - 1)

        RG, RH = reach(REACH, LX, n_gx), reach(REACH, LY, n_yz)
        WG = n_gx if n_gx <= 2 * RG + 1 else 2 * RG + 1
        WH = n_yz if n_yz <= 2 * RH + 1 else 2 * RH + 1
        cfg = (n_grp, n_gx, n_yz, LX, LY, LZ, WG, WH, RG, RH)
        spec = (P("gx", "yz", "grp", None), P("gx", "yz", "grp"), P("gx", "yz", "grp"), P(), P())
        run = jax.shard_map(
            functools.partial(body, cfg), mesh=mesh, in_specs=spec,
            out_specs=P("gx", "yz", "grp", None), check_vma=False,
        )
        return run(rhs, coeff, flags, basis, eigenvalues)

    return call
```

```python
import functools

import jax
import jax.numpy as jnp
import numpy as np
from jax import lax
from jax.experimental import pallas as pl
from jax.experimental.pallas import tpu as pltpu
from jax.sharding import PartitionSpec as P

DEG1 = 8
NODES = 512
CHEB = 4
CHEB_LOW = 0.1
CHEB_HIGH = 2.0
REACH = 7
REACH_FACE = 4
GLL_POINTS = (
    -1.0,
    -0.8717401485096066,
    -0.5917001814331423,
    -0.2092992179024789,
    0.2092992179024789,
    0.5917001814331423,
    0.8717401485096066,
    1.0,
)
L0 = [(1.0 - x) * 0.5 for x in GLL_POINTS]
L1 = [(1.0 + x) * 0.5 for x in GLL_POINTS]
MASS_SAME = sum(a * a for a in L0)
MASS_OTHER = sum(a * b for a, b in zip(L0, L1))
MESH = pl.DeviceIdType.MESH
F32 = jnp.float32
BF16 = jnp.bfloat16


def iota(shape, dim):
    return lax.broadcasted_iota(jnp.int32, shape, dim)


def parts_of(x, count):
    found = []
    for _ in range(count):
        head = x.astype(BF16)
        found.append(head)
        x = x - head.astype(F32)
    return found


def dot(a, b, dims=((1,), (0,)), parts=(2, 2)):
    pa, pb = parts_of(a, parts[0]), parts_of(b, parts[1])
    order = max(parts)
    out = None
    for p in range(parts[0]):
        for q in range(parts[1]):
            if p + q < order:
                term = lax.dot_general(pa[p], pb[q], (dims, ((), ())), preferred_element_type=F32)
                out = term if out is None else out + term
    return out


def split(x):
    hi = x.astype(BF16)
    return hi, (x - hi.astype(F32)).astype(BF16)


def dot3(x, hi, lo):
    xh, xl = split(x)
    rows = x.shape[0]
    both = jnp.dot(jnp.concatenate([xh, xl], axis=0), hi, preferred_element_type=F32)
    return both[:rows] + (both[rows:] + jnp.dot(xh, lo, preferred_element_type=F32))


def pick(index, table):
    out = jnp.full(index.shape, table[0], F32)
    for i in range(1, len(table)):
        out = jnp.where(index == i, table[i], out)
    return out


def kernel(
    cfg,
    rhs_hbm, coeff_hbm, flags_hbm, basis_hbm, eig_hbm,
    out_ref,
    rhs_ref, coeff_ref, flags_ref, basis_ref, eig_ref,
    mine_b, other_b, mine_p, other_p, win_b, win_p, planes, cfx, ext3, ext1,
    rhs_s, s_ref, e_hi, e_lo, t_hi, t_lo,
    ysend, yrecv, zsend, zrecv, xrecv, nb,
    in_sem, b_send, b_recv, p_send, p_recv, g_send, g_recv, fsend, frecv,
):
    n_grp, n_gx, n_yz, LX, LY, LZ, WG, WH, RG, RH = cfg
    LT = planes.shape[0]
    L = LT * 128
    XP = cfx.shape[1]
    FROWS = XP * 8
    me_grp = lax.axis_index("grp")
    me_gx = lax.axis_index("gx")
    me_yz = lax.axis_index("yz")
    full_g = WG == n_gx
    full_h = WH == n_yz
    gs = me_gx if full_g else RG
    hs = me_yz if full_h else RH
    g_start = 0 if full_g else me_gx - RG
    h_start = 0 if full_h else me_yz - RH

    loads = []
    pairs_in = [
        (basis_hbm, basis_ref), (eig_hbm, eig_ref), (rhs_hbm, rhs_ref),
        (coeff_hbm, coeff_ref), (flags_hbm, flags_ref),
    ]
    for n, (src, dst) in enumerate(pairs_in):
        load = pltpu.make_async_copy(src, dst, in_sem.at[n])
        load.start()
        loads.append(load)
    win_b[...] = jnp.zeros(win_b.shape, F32)
    win_p[...] = jnp.zeros(win_p.shape, F32)

    me_of = {"grp": me_grp, "gx": me_gx, "yz": me_yz}
    n_of = {"grp": n_grp, "gx": n_gx, "yz": n_yz}

    def exists(axis, k):
        at = me_of[axis] + k
        return jnp.logical_and(at >= 0, at < n_of[axis])

    def cost(k, local):
        return 0 if k == 0 else (abs(k) - 1) * local + 1

    def around(reach):
        return [
            (kg, kh)
            for kg in range(-RG, RG + 1)
            for kh in range(-RH, RH + 1)
            if (kg, kh) != (0, 0) and cost(kg, LX) + cost(kh, LY) <= reach
        ]

    def target(key):
        return {axis: me_of[axis] + k for axis, k in key if k}

    def present(key):
        there = None
        for axis, k in key:
            if k:
                here = exists(axis, k)
                there = here if there is None else jnp.logical_and(there, here)
        return there

    grp_keys = [(("grp", k),) for k in (-1, 1)] if n_grp > 1 else []
    b_keys = [(("gx", kg), ("yz", kh)) for kg, kh in around(REACH)]
    p_keys = [(("gx", kg), ("yz", kh)) for kg, kh in around(REACH_FACE)]

    barrier = pltpu.get_barrier_semaphore()
    count = jnp.int32(0)
    for key in grp_keys + b_keys:
        here = present(key)
        count = count + here.astype(jnp.int32)

        @pl.when(here)
        def _(key=key):
            pl.semaphore_signal(barrier, inc=1, device_id=target(key), device_id_type=MESH)

    lane = iota((8, NODES), 1)
    sub = iota((8, NODES), 0)
    v1 = (lane // 64 == sub).astype(F32)
    v2 = ((lane // 8) % 8 == sub).astype(F32)
    v3 = (lane % 8 == sub).astype(F32)

    node_at = (lane // 64, (lane // 8) % 8, lane % 8)
    side_at = (sub // 4, (sub // 2) % 2, sub % 2)
    restrict = jnp.ones((8, NODES), F32)
    for d in range(3):
        restrict = restrict * jnp.where(side_at[d] == 0, pick(node_at[d], L0), pick(node_at[d], L1))
    on_face = [
        jnp.where(node_at[d] == 7 * side_at[d], restrict, 0.0) for d in range(3)
    ]
    faces = jnp.concatenate(on_face, axis=0)

    YZ = LY * LZ
    NE = LX * YZ
    row = iota((NE, 1), 0)
    row_x, row_y, row_z = row // YZ, (row // LZ) % LY, row % LZ
    ysel = (iota((YZ, LY), 0) // LZ == iota((YZ, LY), 1)).astype(F32)
    zsel = iota((YZ, LZ), 0) % LZ == iota((YZ, LZ), 1)

    r16 = iota((YZ, 128), 0)
    l16 = iota((YZ, 128), 1)
    spot = (r16 // LZ) * 8 + me_grp * LZ + r16 % LZ
    tail = (l16 == 96 + spot).astype(F32)
    re = iota((NE, 128), 0)
    place = (
        iota((NE, 128), 1) == (re // YZ) * 32 + ((re // LZ) % LY) * 8 + me_grp * LZ + re % LZ
    ).astype(F32)

    for load in loads[2:]:
        load.wait()
    for x in range(LX):
        for y in range(LY):
            at = x * YZ + y * LZ
            rhs_s[at : at + LZ, :] = rhs_ref[x, y]
    rhs = rhs_s[...]
    def column(ref):
        parts = []
        for x in range(LX):
            spread = dot(ysel, ref[x].astype(F32), parts=(1, 3))
            parts.append(jnp.sum(jnp.where(zsel, spread, 0.0), axis=1, keepdims=True))
        return parts

    coeff_cols = column(coeff_ref)
    flag_cols = column(flags_ref)
    coeff_col = jnp.concatenate(coeff_cols, axis=0)
    flag_col = jnp.concatenate(flag_cols, axis=0)

    b_own = dot(dot(restrict, rhs, ((1,), (1,))), place, parts=(2, 1))
    row8 = iota((8, 128), 0)
    for x in range(LX):
        c_line = jnp.sum(coeff_cols[x] * tail, axis=0, keepdims=True)
        f_line = jnp.sum(flag_cols[x] * tail, axis=0, keepdims=True)
        b_own = b_own + jnp.where(row8 == x, c_line, 0.0) + jnp.where(row8 == LX + x, f_line, 0.0)
    mine_b[...] = b_own

    def remote(src, dst, send, recv, n, key):
        copy = pltpu.make_async_remote_copy(
            src_ref=src, dst_ref=dst, send_sem=send.at[n], recv_sem=recv.at[n],
            device_id=target(key), device_id_type=MESH,
        )
        return key, copy

    def around_copies(ref, keys, send, recv):
        found = []
        for n, key in enumerate(keys):
            kg, kh = key[0][1], key[1][1]
            slot = (hs if full_h else RH - kh, gs if full_g else RG - kg)
            found.append(remote(ref.at[hs, gs], ref.at[slot[0], slot[1]], send, recv, n, key))
        return found

    def start_all(copies):
        for key, copy in copies:
            @pl.when(present(key))
            def _(copy=copy):
                copy.start()

    def wait_recv(copies):
        for key, copy in copies:
            @pl.when(present([(axis, -k) for axis, k in key]))
            def _(copy=copy):
                copy.wait_recv()

    def wait_send(copies):
        for key, copy in copies:
            @pl.when(present(key))
            def _(copy=copy):
                copy.wait_send()

    grp_b = [remote(mine_b, other_b, g_send, g_recv, n, key) for n, key in enumerate(grp_keys)]
    grp_p = [remote(mine_p, other_p, g_send, g_recv, 2 + n, key) for n, key in enumerate(grp_keys)]
    all_b = around_copies(win_b, b_keys, b_send, b_recv)
    all_p = around_copies(win_p, p_keys, p_send, p_recv)

    pl.semaphore_wait(barrier, count)
    start_all(grp_b)
    loads[0].wait()
    loads[1].wait()
    basis = basis_ref[...]

    def build(hi_ref, lo_ref, dims):
        t1 = dot(basis, v1, dims, (3, 1))
        t2 = dot(basis, v2, dims, (3, 1))
        t3 = dot(basis, v3, dims, (3, 1))
        pairs = jnp.concatenate([t2[j : j + 1, :] * t3 for j in range(8)], axis=0)
        for i in range(8):
            hi, lo = split(t1[i : i + 1, :] * pairs)
            hi_ref[i * 64 : (i + 1) * 64, :] = hi
            lo_ref[i * 64 : (i + 1) * 64, :] = lo

    build(e_hi, e_lo, ((1,), (0,)))
    build(t_hi, t_lo, ((0,), (0,)))
    spectrum = dot(eig_ref[...], v1 + v2 + v3, parts=(3, 1))

    inverse = 1.0 / (coeff_col * spectrum)
    s = dot3(dot3(rhs, e_hi[...], e_lo[...]) * inverse, t_hi[...], t_lo[...])
    s_ref[...] = s
    wait_recv(grp_b)
    win_b[hs, gs] = mine_b[...] + other_b[...] if n_grp > 1 else mine_b[...]
    start_all(all_b)
    mine_p[...] = dot(dot(faces, s, ((1,), (1,))), place, parts=(2, 1))
    start_all(grp_p)

    for side in range(2):
        yy, zz = (0, 0) if side == 0 else (LY - 1, LZ - 1)
        for x in range(LX):
            ysend[side, x * LZ : (x + 1) * LZ, :] = s_ref[x * YZ + yy * LZ : x * YZ + (yy + 1) * LZ, :]
            for y in range(LY):
                at = x * YZ + y * LZ + zz
                zsend[side, x * LY + y : x * LY + y + 1, :] = s_ref[at : at + 1, :]

    def face_copies():
        found = []
        for n, (axis, k) in enumerate(
            [("gx", -1), ("gx", 1), ("yz", -1), ("yz", 1), ("grp", -1), ("grp", 1)]
        ):
            if n_of[axis] == 1:
                continue
            side = 0 if k < 0 else 1
            if axis == "gx":
                at = 0 if side == 0 else (LX - 1) * YZ
                src, dst = s_ref.at[pl.ds(at, YZ)], xrecv.at[1 - side]
            elif axis == "yz":
                src, dst = ysend.at[side], yrecv.at[1 - side]
            else:
                src, dst = zsend.at[side], zrecv.at[1 - side]
            found.append(remote(src, dst, fsend, frecv, n, ((axis, k),)))
        return found

    next_door = face_copies()
    start_all(next_door)
    wait_recv(grp_p)
    win_p[hs, gs] = mine_p[...] + other_p[...] if n_grp > 1 else mine_p[...]
    start_all(all_p)
    planes[...] = jnp.zeros(planes.shape, F32)
    cfx[...] = jnp.zeros(cfx.shape, F32)
    wait_recv(next_door)

    own_at = (me_gx * LX + row_x, me_yz * LY + row_y, me_grp * LZ + row_z)
    totals = (n_gx * LX, n_yz * LY, n_grp * LZ)
    node_lane = iota((1, NODES), 1)
    node_of = (node_lane // 64, (node_lane // 8) % 8, node_lane % 8)
    strides = (64, 8, 1)
    face_s = jnp.zeros((NE, NODES), F32)
    for d in range(3):
        for side in range(2):
            if d == 0:
                if side == 0:
                    beside = jnp.concatenate([xrecv[0], s[: NE - YZ]], axis=0)
                else:
                    beside = jnp.concatenate([s[YZ:], xrecv[1]], axis=0)
            else:
                step = LZ if d == 1 else 1
                nb[...] = pltpu.roll(s, step if side == 0 else NE - step, 0)
                for x in range(LX):
                    if d == 1:
                        at = x * YZ + (0 if side == 0 else (LY - 1) * LZ)
                        nb[at : at + LZ, :] = yrecv[side, x * LZ : (x + 1) * LZ, :]
                    else:
                        for y in range(LY):
                            at = x * YZ + y * LZ + (0 if side == 0 else LZ - 1)
                            nb[at : at + 1, :] = zrecv[side, x * LY + y : x * LY + y + 1, :]
                beside = nb[...]
            has = own_at[d] > 0 if side == 0 else own_at[d] < totals[d] - 1
            gain = jnp.where(has, 1.0, flag_col)
            shift = 7 * strides[d]
            moved = pltpu.roll(beside, NODES - shift if side == 0 else shift, 1)
            term = gain * s - jnp.where(has, moved, 0.0)
            face_s = face_s + jnp.where(node_of[d] == 7 * side, term, 0.0)

    wait_recv(all_b)

    def spread(win, rows, first_field):
        lane_slot = iota((rows, L), 1) // 32
        for g in range(WG):
            cf_plane = jnp.zeros((rows, L), F32)
            tiles = []
            for h in range(WH):
                tile = win[h, g]
                if L > 128:
                    tile = jnp.concatenate([tile, jnp.zeros((rows, L - 128), F32)], axis=1)
                tiles.append(tile)
                if first_field == 0:
                    moved = pltpu.roll(tile, (32 * (h - 3)) % L, 1)
                    cf_plane = jnp.where(lane_slot == h, moved, cf_plane)
            for x in range(LX):
                plane = jnp.zeros((rows, L), F32)
                for h in range(WH):
                    amount = (32 * (h - x)) % L
                    moved = pltpu.roll(tiles[h], amount, 1) if amount else tiles[h]
                    plane = jnp.where(lane_slot == h, moved, plane)
                at = (g * LX + x) * 8
                for f in range(rows // 8):
                    to = (first_field + f) * FROWS + at
                    for t in range(LT):
                        part = plane[f * 8 : f * 8 + 8, t * 128 : (t + 1) * 128]
                        planes[t, to : to + 8, :] = part
            if first_field == 0:
                cfx[0, g * LX : (g + 1) * LX, :] = cf_plane[0:LX]
                cfx[1, g * LX : (g + 1) * LX, :] = cf_plane[LX : 2 * LX]

    spread(win_b, 8, 0)

    def strided(ref, start, stride):
        parts = [ref[t, pl.ds(start, XP, stride=stride), :] for t in range(LT)]
        return parts[0] if LT == 1 else jnp.concatenate(parts, axis=1)

    def store_strided(ref, start, stride, value):
        for t in range(LT):
            ref[t, pl.ds(start, XP, stride=stride), :] = value[:, t * 128 : (t + 1) * 128]

    def field(f):
        return [strided(planes, f * FROWS + a, 8) for a in range(8)]

    rhs1 = field(0)
    coeff = cfx[0]
    flag = cfx[1]
    pos = (
        g_start * LX + iota((XP, L), 0),
        h_start * LY + iota((XP, L), 1) // 8,
        iota((XP, L), 1) % 8,
    )
    has = [(pos[d] > 0, pos[d] < totals[d] - 1) for d in range(3)]
    gain = [[jnp.where(has[d][q], 1.0, flag) for q in range(2)] for d in range(3)]
    roll_axis = (0, 1, 1)
    roll_step = (1, 8, 1)
    bit = (4, 2, 1)

    def side_of(a, d):
        return (a // bit[d]) % 2

    def beside_of(v, a, d):
        q = side_of(a, d)
        size = XP if d == 0 else L
        step = roll_step[d] if q == 0 else size - roll_step[d]
        return jnp.where(has[d][q], pltpu.roll(v[a ^ bit[d]], step, roll_axis[d]), 0.0)

    def jump(v, a, d):
        return gain[d][side_of(a, d)] * v[a] - beside_of(v, a, d)

    diag = [
        coeff * 3.5 + gain[0][side_of(a, 0)] + gain[1][side_of(a, 1)] + gain[2][side_of(a, 2)]
        for a in range(8)
    ]

    def coarse_apply(v):
        out = []
        for a in range(8):
            flips = v[a ^ 4] + v[a ^ 2] + v[a ^ 1]
            sides = beside_of(v, a, 0) + beside_of(v, a, 1) + beside_of(v, a, 2)
            out.append(diag[a] * v[a] - coeff * flips - sides)
        return out

    center = 0.5 * (CHEB_HIGH + CHEB_LOW)
    half_width = 0.5 * (CHEB_HIGH - CHEB_LOW)
    inverse_diag = 1.0 / (coeff * 3.5 + 3.0)

    def cheb(f):
        sigma = center / half_width
        rho = 1.0 / sigma
        remain = f
        first = inverse_diag * (1.0 / center)
        update = [first * r for r in remain]
        result = update
        for _ in range(CHEB - 1):
            applied = coarse_apply(update)
            remain = [r - t for r, t in zip(remain, applied)]
            rho_next = 1.0 / (2.0 * sigma - rho)
            weight = inverse_diag * (2.0 * rho_next / half_width)
            update = [(rho_next * rho) * u + weight * r for u, r in zip(update, remain)]
            result = [t + u for t, u in zip(result, update)]
            rho = rho_next
        return result

    col = iota((8, 8), 0)
    w = [jnp.sum(pick(col, t) * basis, axis=0, keepdims=True) for t in (L0, L1)]
    eig = eig_ref[...]
    stiff = [[jnp.sum(eig * w[p] * w[q], axis=1, keepdims=True) for q in range(2)] for p in range(2)]

    def mass(v, d):
        return [MASS_SAME * v[a] + MASS_OTHER * v[a ^ bit[d]] for a in range(8)]

    c1 = cheb(rhs1)
    m3 = mass(c1, 2)
    m23 = mass(m3, 1)
    m13 = mass(m3, 0)
    m12 = mass(mass(c1, 1), 0)
    masses = (m23, m13, m12)
    rhs2 = []
    for a in range(8):
        inner = 0.0
        for d in range(3):
            q = side_of(a, d)
            inner = inner + stiff[q][q] * masses[d][a] + stiff[q][1 - q] * masses[d][a ^ bit[d]]
        rhs2.append(0.5 * rhs1[a] - 0.5 * coeff * inner)
    first_row = gs * LX
    absolute = hs * 32 + (iota((YZ, L), 0) // LZ) * 8 + me_grp * LZ + iota((YZ, L), 0) % LZ
    take = (iota((YZ, L), 1) == absolute).astype(F32)

    def own_values(ref, comps):
        parts = []
        for x in range(LX):
            start = pl.multiple_of((first_row + x) * comps, 8)
            part = 0.0
            for t in range(LT):
                lanes = take[:, t * 128 : (t + 1) * 128]
                part = part + dot(lanes, ref[t, pl.ds(start, comps), :], ((1,), (1,)), (1, 2))
            parts.append(part)
        return jnp.concatenate(parts, axis=0)

    for d in range(3):
        for a in range(8):
            store_strided(ext3, d * 8 + a, 24, jump(c1, a, d))
    face_c = dot(own_values(ext3, 24), faces)
    total = face_s + face_c
    smooth2 = dot3(dot3(total, e_hi[...], e_lo[...]) * inverse, t_hi[...], t_lo[...])

    wait_recv(all_p)
    spread(win_p, 24, 1)
    proj = [field(1 + d) for d in range(3)]
    for d in range(3):
        both = [proj[d][a] + masses[d][a] for a in range(8)]
        rhs2 = [rhs2[a] - jump(both, a, d) for a in range(8)]
    c2 = cheb(rhs2)
    for a in range(8):
        store_strided(ext1, a, 8, 0.25 * c1[a] + 0.5 * c2[a])
    lifted = dot(own_values(ext1, 8), restrict)
    out_ref[...] = 0.75 * s + lifted - 0.5 * smooth2

    for copies in (grp_b, grp_p, all_b, all_p, next_door):
        wait_send(copies)


def body(cfg, rhs, coeff, flags, basis, eigenvalues):
    n_grp, n_gx, n_yz, LX, LY, LZ, WG, WH, RG, RH = cfg
    NE = LX * LY * LZ
    L = -(-(WH * 32) // 128) * 128
    XP = -(-(WG * LX) // 8) * 8
    V = pltpu.VMEM
    n_peers = (2 * RG + 1) * (2 * RH + 1)
    out = pl.pallas_call(
        functools.partial(kernel, cfg),
        out_shape=V((NE, NODES), F32),
        in_specs=[pl.BlockSpec(memory_space=pltpu.HBM)] * 5,
        out_specs=pl.BlockSpec(memory_space=V),
        scratch_shapes=[
            V(rhs.shape, F32),
            V(coeff.shape, F32),
            V(flags.shape, jnp.int32),
            V(basis.shape, F32),
            V((1, DEG1), F32),
            V((8, 128), F32),
            V((8, 128), F32),
            V((24, 128), F32),
            V((24, 128), F32),
            V((WH, WG, 8, 128), F32),
            V((WH, WG, 24, 128), F32),
            V((L // 128, 4 * XP * 8, 128), F32),
            V((2, XP, L), F32),
            V((L // 128, XP * 24, 128), F32),
            V((L // 128, XP * 8, 128), F32),
            V((NE, NODES), F32),
            V((NE, NODES), F32),
            V((NODES, NODES), BF16),
            V((NODES, NODES), BF16),
            V((NODES, NODES), BF16),
            V((NODES, NODES), BF16),
            V((2, 16, NODES), F32),
            V((2, 16, NODES), F32),
            V((2, 16, NODES), F32),
            V((2, 16, NODES), F32),
            V((2, LY * LZ, NODES), F32),
            V((NE, NODES), F32),
            pltpu.SemaphoreType.DMA((5,)),
            pltpu.SemaphoreType.DMA((n_peers,)),
            pltpu.SemaphoreType.DMA((n_peers,)),
            pltpu.SemaphoreType.DMA((n_peers,)),
            pltpu.SemaphoreType.DMA((n_peers,)),
            pltpu.SemaphoreType.DMA((4,)),
            pltpu.SemaphoreType.DMA((4,)),
            pltpu.SemaphoreType.DMA((6,)),
            pltpu.SemaphoreType.DMA((6,)),
        ],
        compiler_params=pltpu.CompilerParams(
            collective_id=0, has_side_effects=True, vmem_limit_bytes=60 * 1024 * 1024
        ),
    )(rhs, coeff, flags, basis, eigenvalues.reshape(1, DEG1))
    return out.reshape(rhs.shape)


def solution(mesh):
    n_grp, n_gx, n_yz = (mesh.shape[a] for a in ("grp", "gx", "yz"))

    def call(rhs, coeff, flags, basis, eigenvalues):
        EX, EY, EZ = rhs.shape[:3]
        LX, LY, LZ = EX // n_gx, EY // n_yz, EZ // n_grp
        assert LX <= 3 and LY <= 4 and EZ <= 8 and n_grp <= 2

        def reach(steps, local, count):
            return min(-(-steps // local), count - 1)

        RG, RH = reach(REACH, LX, n_gx), reach(REACH, LY, n_yz)
        WG = n_gx if n_gx <= 2 * RG + 1 else 2 * RG + 1
        WH = n_yz if n_yz <= 2 * RH + 1 else 2 * RH + 1
        cfg = (n_grp, n_gx, n_yz, LX, LY, LZ, WG, WH, RG, RH)
        spec = (P("gx", "yz", "grp", None), P("gx", "yz", "grp"), P("gx", "yz", "grp"), P(), P())
        run = jax.shard_map(
            functools.partial(body, cfg), mesh=mesh, in_specs=spec,
            out_specs=P("gx", "yz", "grp", None), check_vma=False,
        )
        return run(rhs, coeff, flags, basis, eigenvalues)

    return call
```

```python
import functools

import jax
import jax.numpy as jnp
import numpy as np
from jax import lax
from jax.experimental import pallas as pl
from jax.experimental.pallas import tpu as pltpu
from jax.sharding import PartitionSpec as P

DEG1 = 8
NODES = 512
CHEB = 4
CHEB_LOW = 0.1
CHEB_HIGH = 2.0
REACH = 7
REACH_FACE = 4
GLL_POINTS = (
    -1.0,
    -0.8717401485096066,
    -0.5917001814331423,
    -0.2092992179024789,
    0.2092992179024789,
    0.5917001814331423,
    0.8717401485096066,
    1.0,
)
L0 = [(1.0 - x) * 0.5 for x in GLL_POINTS]
L1 = [(1.0 + x) * 0.5 for x in GLL_POINTS]
MASS_SAME = sum(a * a for a in L0)
MASS_OTHER = sum(a * b for a, b in zip(L0, L1))
MESH = pl.DeviceIdType.MESH
F32 = jnp.float32
BF16 = jnp.bfloat16


def iota(shape, dim):
    return lax.broadcasted_iota(jnp.int32, shape, dim)


def parts_of(x, count):
    found = []
    for _ in range(count):
        head = x.astype(BF16)
        found.append(head)
        x = x - head.astype(F32)
    return found


def dot(a, b, dims=((1,), (0,)), parts=(2, 2)):
    pa, pb = parts_of(a, parts[0]), parts_of(b, parts[1])
    order = max(parts)
    out = None
    for p in range(parts[0]):
        for q in range(parts[1]):
            if p + q < order:
                term = lax.dot_general(pa[p], pb[q], (dims, ((), ())), preferred_element_type=F32)
                out = term if out is None else out + term
    return out


def split(x):
    hi = x.astype(BF16)
    return hi, (x - hi.astype(F32)).astype(BF16)


def dot3(x, hi, lo):
    xh, xl = split(x)
    rows = x.shape[0]
    both = jnp.dot(jnp.concatenate([xh, xl], axis=0), hi, preferred_element_type=F32)
    return both[:rows] + (both[rows:] + jnp.dot(xh, lo, preferred_element_type=F32))


def pick(index, table):
    out = jnp.full(index.shape, table[0], F32)
    for i in range(1, len(table)):
        out = jnp.where(index == i, table[i], out)
    return out


def kernel(
    cfg,
    rhs_hbm, coeff_hbm, flags_hbm, basis_hbm, eig_hbm,
    out_ref,
    rhs_ref, coeff_ref, flags_ref, basis_ref, eig_ref,
    mine_b, other_b, mine_p, other_p, win_b, win_p, planes, cfx, ext3, ext1,
    rhs_s, s_ref, e_hi, e_lo, t_hi, t_lo,
    ysend, yrecv, zsend, zrecv, xrecv, nb,
    in_sem, b_send, b_recv, p_send, p_recv, g_send, g_recv, fsend, frecv,
):
    n_grp, n_gx, n_yz, LX, LY, LZ, WG, WH, RG, RH = cfg
    LT = planes.shape[0]
    L = LT * 128
    XP = cfx.shape[1]
    FROWS = XP * 8
    me_grp = lax.axis_index("grp")
    me_gx = lax.axis_index("gx")
    me_yz = lax.axis_index("yz")
    full_g = WG == n_gx
    full_h = WH == n_yz
    gs = me_gx if full_g else RG
    hs = me_yz if full_h else RH
    g_start = 0 if full_g else me_gx - RG
    h_start = 0 if full_h else me_yz - RH

    loads = []
    pairs_in = [
        (basis_hbm, basis_ref), (eig_hbm, eig_ref), (rhs_hbm, rhs_ref),
        (coeff_hbm, coeff_ref), (flags_hbm, flags_ref),
    ]
    for n, (src, dst) in enumerate(pairs_in):
        load = pltpu.make_async_copy(src, dst, in_sem.at[n])
        load.start()
        loads.append(load)
    win_b[...] = jnp.zeros(win_b.shape, F32)
    win_p[...] = jnp.zeros(win_p.shape, F32)

    me_of = {"grp": me_grp, "gx": me_gx, "yz": me_yz}
    n_of = {"grp": n_grp, "gx": n_gx, "yz": n_yz}

    def exists(axis, k):
        at = me_of[axis] + k
        return jnp.logical_and(at >= 0, at < n_of[axis])

    def cost(k, local):
        return 0 if k == 0 else (abs(k) - 1) * local + 1

    def around(reach):
        return [
            (kg, kh)
            for kg in range(-RG, RG + 1)
            for kh in range(-RH, RH + 1)
            if (kg, kh) != (0, 0) and cost(kg, LX) + cost(kh, LY) <= reach
        ]

    def target(key):
        return {axis: me_of[axis] + k for axis, k in key if k}

    def present(key):
        there = None
        for axis, k in key:
            if k:
                here = exists(axis, k)
                there = here if there is None else jnp.logical_and(there, here)
        return there

    grp_keys = [(("grp", k),) for k in (-1, 1)] if n_grp > 1 else []
    gx_keys = [(("gx", k),) for k in range(-RG, RG + 1) if k]
    yz_keys = [(("yz", k),) for k in range(-RH, RH + 1) if k]
    p_keys = [(("gx", kg), ("yz", kh)) for kg, kh in around(REACH_FACE)]

    barrier = pltpu.get_barrier_semaphore()
    count = jnp.int32(0)
    diagonal = [key for key in p_keys if key[0][1] and key[1][1]]
    for key in grp_keys + gx_keys + yz_keys + diagonal:
        here = present(key)
        count = count + here.astype(jnp.int32)

        @pl.when(here)
        def _(key=key):
            pl.semaphore_signal(barrier, inc=1, device_id=target(key), device_id_type=MESH)

    lane = iota((8, NODES), 1)
    sub = iota((8, NODES), 0)
    v1 = (lane // 64 == sub).astype(F32)
    v2 = ((lane // 8) % 8 == sub).astype(F32)
    v3 = (lane % 8 == sub).astype(F32)

    node_at = (lane // 64, (lane // 8) % 8, lane % 8)
    side_at = (sub // 4, (sub // 2) % 2, sub % 2)
    restrict = jnp.ones((8, NODES), F32)
    for d in range(3):
        restrict = restrict * jnp.where(side_at[d] == 0, pick(node_at[d], L0), pick(node_at[d], L1))
    on_face = [
        jnp.where(node_at[d] == 7 * side_at[d], restrict, 0.0) for d in range(3)
    ]
    faces = jnp.concatenate(on_face, axis=0)

    YZ = LY * LZ
    NE = LX * YZ
    row = iota((NE, 1), 0)
    row_x, row_y, row_z = row // YZ, (row // LZ) % LY, row % LZ
    ysel = (iota((YZ, LY), 0) // LZ == iota((YZ, LY), 1)).astype(F32)
    zsel = iota((YZ, LZ), 0) % LZ == iota((YZ, LZ), 1)

    r16 = iota((YZ, 128), 0)
    l16 = iota((YZ, 128), 1)
    spot = (r16 // LZ) * 8 + me_grp * LZ + r16 % LZ
    tail = (l16 == 96 + spot).astype(F32)
    re = iota((NE, 128), 0)
    place = (
        iota((NE, 128), 1) == (re // YZ) * 32 + ((re // LZ) % LY) * 8 + me_grp * LZ + re % LZ
    ).astype(F32)

    for load in loads[2:]:
        load.wait()
    for x in range(LX):
        for y in range(LY):
            at = x * YZ + y * LZ
            rhs_s[at : at + LZ, :] = rhs_ref[x, y]
    rhs = rhs_s[...]
    def column(ref):
        parts = []
        for x in range(LX):
            spread = dot(ysel, ref[x].astype(F32), parts=(1, 3))
            parts.append(jnp.sum(jnp.where(zsel, spread, 0.0), axis=1, keepdims=True))
        return parts

    coeff_cols = column(coeff_ref)
    flag_cols = column(flags_ref)
    coeff_col = jnp.concatenate(coeff_cols, axis=0)
    flag_col = jnp.concatenate(flag_cols, axis=0)

    b_own = dot(dot(restrict, rhs, ((1,), (1,))), place, parts=(2, 1))
    row8 = iota((8, 128), 0)
    for x in range(LX):
        c_line = jnp.sum(coeff_cols[x] * tail, axis=0, keepdims=True)
        f_line = jnp.sum(flag_cols[x] * tail, axis=0, keepdims=True)
        b_own = b_own + jnp.where(row8 == x, c_line, 0.0) + jnp.where(row8 == LX + x, f_line, 0.0)
    mine_b[...] = b_own

    def remote(src, dst, send, recv, n, key):
        copy = pltpu.make_async_remote_copy(
            src_ref=src, dst_ref=dst, send_sem=send.at[n], recv_sem=recv.at[n],
            device_id=target(key), device_id_type=MESH,
        )
        return key, copy

    def around_copies(ref, keys, send, recv):
        found = []
        for n, key in enumerate(keys):
            kg, kh = key[0][1], key[1][1]
            slot = (hs if full_h else RH - kh, gs if full_g else RG - kg)
            found.append(remote(ref.at[hs, gs], ref.at[slot[0], slot[1]], send, recv, n, key))
        return found

    def start_all(copies):
        for key, copy in copies:
            @pl.when(present(key))
            def _(copy=copy):
                copy.start()

    def wait_recv(copies):
        for key, copy in copies:
            @pl.when(present([(axis, -k) for axis, k in key]))
            def _(copy=copy):
                copy.wait_recv()

    def wait_send(copies):
        for key, copy in copies:
            @pl.when(present(key))
            def _(copy=copy):
                copy.wait_send()

    grp_b = [remote(mine_b, other_b, g_send, g_recv, n, key) for n, key in enumerate(grp_keys)]
    grp_p = [remote(mine_p, other_p, g_send, g_recv, 2 + n, key) for n, key in enumerate(grp_keys)]
    gx_b, yz_b = [], []
    for n, key in enumerate(gx_keys):
        slot = gs if full_g else RG - key[0][1]
        gx_b.append(remote(win_b.at[hs, gs], win_b.at[hs, slot], b_send, b_recv, n, key))
    for n, key in enumerate(yz_keys):
        slot = hs if full_h else RH - key[0][1]
        yz_b.append(remote(win_b.at[hs], win_b.at[slot], b_send, b_recv, len(gx_keys) + n, key))
    all_p = around_copies(win_p, p_keys, p_send, p_recv)

    pl.semaphore_wait(barrier, count)
    start_all(grp_b)
    loads[0].wait()
    loads[1].wait()
    basis = basis_ref[...]

    def build(hi_ref, lo_ref, dims):
        t1 = dot(basis, v1, dims, (3, 1))
        t2 = dot(basis, v2, dims, (3, 1))
        t3 = dot(basis, v3, dims, (3, 1))
        pairs = jnp.concatenate([t2[j : j + 1, :] * t3 for j in range(8)], axis=0)
        for i in range(8):
            hi, lo = split(t1[i : i + 1, :] * pairs)
            hi_ref[i * 64 : (i + 1) * 64, :] = hi
            lo_ref[i * 64 : (i + 1) * 64, :] = lo

    build(e_hi, e_lo, ((1,), (0,)))
    build(t_hi, t_lo, ((0,), (0,)))
    spectrum = dot(eig_ref[...], v1 + v2 + v3, parts=(3, 1))

    inverse = 1.0 / (coeff_col * spectrum)
    wait_recv(grp_b)
    win_b[hs, gs] = mine_b[...] + other_b[...] if n_grp > 1 else mine_b[...]
    start_all(gx_b)
    inside = dot3(rhs, e_hi[...], e_lo[...])
    wait_recv(gx_b)
    start_all(yz_b)
    s = dot3(inside * inverse, t_hi[...], t_lo[...])
    s_ref[...] = s
    mine_p[...] = dot(dot(faces, s, ((1,), (1,))), place, parts=(2, 1))
    start_all(grp_p)

    for side in range(2):
        yy, zz = (0, 0) if side == 0 else (LY - 1, LZ - 1)
        for x in range(LX):
            ysend[side, x * LZ : (x + 1) * LZ, :] = s_ref[x * YZ + yy * LZ : x * YZ + (yy + 1) * LZ, :]
            for y in range(LY):
                at = x * YZ + y * LZ + zz
                zsend[side, x * LY + y : x * LY + y + 1, :] = s_ref[at : at + 1, :]

    def face_copies():
        found = []
        for n, (axis, k) in enumerate(
            [("gx", -1), ("gx", 1), ("yz", -1), ("yz", 1), ("grp", -1), ("grp", 1)]
        ):
            if n_of[axis] == 1:
                continue
            side = 0 if k < 0 else 1
            if axis == "gx":
                at = 0 if side == 0 else (LX - 1) * YZ
                src, dst = s_ref.at[pl.ds(at, YZ)], xrecv.at[1 - side]
            elif axis == "yz":
                src, dst = ysend.at[side], yrecv.at[1 - side]
            else:
                src, dst = zsend.at[side], zrecv.at[1 - side]
            found.append(remote(src, dst, fsend, frecv, n, ((axis, k),)))
        return found

    next_door = face_copies()
    start_all(next_door)
    planes[...] = jnp.zeros(planes.shape, F32)
    cfx[...] = jnp.zeros(cfx.shape, F32)
    wait_recv(yz_b)

    def spread(win, rows, first_field):
        lane_slot = iota((rows, L), 1) // 32
        for g in range(WG):
            cf_plane = jnp.zeros((rows, L), F32)
            tiles = []
            for h in range(WH):
                tile = win[h, g]
                if L > 128:
                    tile = jnp.concatenate([tile, jnp.zeros((rows, L - 128), F32)], axis=1)
                tiles.append(tile)
                if first_field == 0:
                    moved = pltpu.roll(tile, (32 * (h - 3)) % L, 1)
                    cf_plane = jnp.where(lane_slot == h, moved, cf_plane)
            for x in range(LX):
                plane = jnp.zeros((rows, L), F32)
                for h in range(WH):
                    amount = (32 * (h - x)) % L
                    moved = pltpu.roll(tiles[h], amount, 1) if amount else tiles[h]
                    plane = jnp.where(lane_slot == h, moved, plane)
                at = (g * LX + x) * 8
                for f in range(rows // 8):
                    to = (first_field + f) * FROWS + at
                    for t in range(LT):
                        part = plane[f * 8 : f * 8 + 8, t * 128 : (t + 1) * 128]
                        planes[t, to : to + 8, :] = part
            if first_field == 0:
                cfx[0, g * LX : (g + 1) * LX, :] = cf_plane[0:LX]
                cfx[1, g * LX : (g + 1) * LX, :] = cf_plane[LX : 2 * LX]

    spread(win_b, 8, 0)

    totals = (n_gx * LX, n_yz * LY, n_grp * LZ)

    def strided(ref, start, stride):
        parts = [ref[t, pl.ds(start, XP, stride=stride), :] for t in range(LT)]
        return parts[0] if LT == 1 else jnp.concatenate(parts, axis=1)

    def store_strided(ref, start, stride, value):
        for t in range(LT):
            ref[t, pl.ds(start, XP, stride=stride), :] = value[:, t * 128 : (t + 1) * 128]

    def field(f):
        return [strided(planes, f * FROWS + a, 8) for a in range(8)]

    rhs1 = field(0)
    coeff = cfx[0]
    flag = cfx[1]
    pos = (
        g_start * LX + iota((XP, L), 0),
        h_start * LY + iota((XP, L), 1) // 8,
        iota((XP, L), 1) % 8,
    )
    has = [(pos[d] > 0, pos[d] < totals[d] - 1) for d in range(3)]
    gain = [[jnp.where(has[d][q], 1.0, flag) for q in range(2)] for d in range(3)]
    roll_axis = (0, 1, 1)
    roll_step = (1, 8, 1)
    bit = (4, 2, 1)

    def side_of(a, d):
        return (a // bit[d]) % 2

    def beside_of(v, a, d):
        q = side_of(a, d)
        size = XP if d == 0 else L
        step = roll_step[d] if q == 0 else size - roll_step[d]
        return jnp.where(has[d][q], pltpu.roll(v[a ^ bit[d]], step, roll_axis[d]), 0.0)

    def jump(v, a, d):
        return gain[d][side_of(a, d)] * v[a] - beside_of(v, a, d)

    diag = [
        coeff * 3.5 + gain[0][side_of(a, 0)] + gain[1][side_of(a, 1)] + gain[2][side_of(a, 2)]
        for a in range(8)
    ]

    def coarse_apply(v):
        out = []
        for a in range(8):
            flips = v[a ^ 4] + v[a ^ 2] + v[a ^ 1]
            sides = beside_of(v, a, 0) + beside_of(v, a, 1) + beside_of(v, a, 2)
            out.append(diag[a] * v[a] - coeff * flips - sides)
        return out

    center = 0.5 * (CHEB_HIGH + CHEB_LOW)
    half_width = 0.5 * (CHEB_HIGH - CHEB_LOW)
    inverse_diag = 1.0 / (coeff * 3.5 + 3.0)

    def cheb(f):
        sigma = center / half_width
        rho = 1.0 / sigma
        remain = f
        first = inverse_diag * (1.0 / center)
        update = [first * r for r in remain]
        result = update
        for _ in range(CHEB - 1):
            applied = coarse_apply(update)
            remain = [r - t for r, t in zip(remain, applied)]
            rho_next = 1.0 / (2.0 * sigma - rho)
            weight = inverse_diag * (2.0 * rho_next / half_width)
            update = [(rho_next * rho) * u + weight * r for u, r in zip(update, remain)]
            result = [t + u for t, u in zip(result, update)]
            rho = rho_next
        return result

    col = iota((8, 8), 0)
    w = [jnp.sum(pick(col, t) * basis, axis=0, keepdims=True) for t in (L0, L1)]
    eig = eig_ref[...]
    stiff = [[jnp.sum(eig * w[p] * w[q], axis=1, keepdims=True) for q in range(2)] for p in range(2)]

    def mass(v, d):
        return [MASS_SAME * v[a] + MASS_OTHER * v[a ^ bit[d]] for a in range(8)]

    c1 = cheb(rhs1)
    wait_recv(grp_p)
    win_p[hs, gs] = mine_p[...] + other_p[...] if n_grp > 1 else mine_p[...]
    start_all(all_p)
    m3 = mass(c1, 2)
    m23 = mass(m3, 1)
    m13 = mass(m3, 0)
    m12 = mass(mass(c1, 1), 0)
    masses = (m23, m13, m12)
    rhs2 = []
    for a in range(8):
        inner = 0.0
        for d in range(3):
            q = side_of(a, d)
            inner = inner + stiff[q][q] * masses[d][a] + stiff[q][1 - q] * masses[d][a ^ bit[d]]
        rhs2.append(0.5 * rhs1[a] - 0.5 * coeff * inner)
    wait_recv(next_door)

    own_at = (me_gx * LX + row_x, me_yz * LY + row_y, me_grp * LZ + row_z)
    node_lane = iota((1, NODES), 1)
    node_of = (node_lane // 64, (node_lane // 8) % 8, node_lane % 8)
    strides = (64, 8, 1)
    face_s = jnp.zeros((NE, NODES), F32)
    for d in range(3):
        for side in range(2):
            if d == 0:
                if side == 0:
                    beside = jnp.concatenate([xrecv[0], s[: NE - YZ]], axis=0)
                else:
                    beside = jnp.concatenate([s[YZ:], xrecv[1]], axis=0)
            else:
                step = LZ if d == 1 else 1
                nb[...] = pltpu.roll(s, step if side == 0 else NE - step, 0)
                for x in range(LX):
                    if d == 1:
                        at = x * YZ + (0 if side == 0 else (LY - 1) * LZ)
                        nb[at : at + LZ, :] = yrecv[side, x * LZ : (x + 1) * LZ, :]
                    else:
                        for y in range(LY):
                            at = x * YZ + y * LZ + (0 if side == 0 else LZ - 1)
                            nb[at : at + 1, :] = zrecv[side, x * LY + y : x * LY + y + 1, :]
                beside = nb[...]
            near = own_at[d] > 0 if side == 0 else own_at[d] < totals[d] - 1
            factor = jnp.where(near, 1.0, flag_col)
            shift = 7 * strides[d]
            moved = pltpu.roll(beside, NODES - shift if side == 0 else shift, 1)
            term = factor * s - jnp.where(near, moved, 0.0)
            face_s = face_s + jnp.where(node_of[d] == 7 * side, term, 0.0)

    first_row = gs * LX
    absolute = hs * 32 + (iota((YZ, L), 0) // LZ) * 8 + me_grp * LZ + iota((YZ, L), 0) % LZ
    take = (iota((YZ, L), 1) == absolute).astype(F32)

    def own_values(ref, comps):
        parts = []
        for x in range(LX):
            start = pl.multiple_of((first_row + x) * comps, 8)
            part = 0.0
            for t in range(LT):
                lanes = take[:, t * 128 : (t + 1) * 128]
                part = part + dot(lanes, ref[t, pl.ds(start, comps), :], ((1,), (1,)), (1, 2))
            parts.append(part)
        return jnp.concatenate(parts, axis=0)

    for d in range(3):
        for a in range(8):
            store_strided(ext3, d * 8 + a, 24, jump(c1, a, d))
    face_c = dot(own_values(ext3, 24), faces)
    total = face_s + face_c
    smooth2 = dot3(dot3(total, e_hi[...], e_lo[...]) * inverse, t_hi[...], t_lo[...])

    wait_recv(all_p)
    spread(win_p, 24, 1)
    proj = [field(1 + d) for d in range(3)]
    for d in range(3):
        both = [proj[d][a] + masses[d][a] for a in range(8)]
        rhs2 = [rhs2[a] - jump(both, a, d) for a in range(8)]
    c2 = cheb(rhs2)
    for a in range(8):
        store_strided(ext1, a, 8, 0.25 * c1[a] + 0.5 * c2[a])
    lifted = dot(own_values(ext1, 8), restrict)
    out_ref[...] = 0.75 * s + lifted - 0.5 * smooth2

    for copies in (grp_b, gx_b, yz_b, grp_p, all_p, next_door):
        wait_send(copies)


def body(cfg, rhs, coeff, flags, basis, eigenvalues):
    n_grp, n_gx, n_yz, LX, LY, LZ, WG, WH, RG, RH = cfg
    NE = LX * LY * LZ
    L = -(-(WH * 32) // 128) * 128
    XP = -(-(WG * LX) // 8) * 8
    V = pltpu.VMEM
    n_peers = (2 * RG + 1) * (2 * RH + 1)
    out = pl.pallas_call(
        functools.partial(kernel, cfg),
        out_shape=V((NE, NODES), F32),
        in_specs=[pl.BlockSpec(memory_space=pltpu.HBM)] * 5,
        out_specs=pl.BlockSpec(memory_space=V),
        scratch_shapes=[
            V(rhs.shape, F32),
            V(coeff.shape, F32),
            V(flags.shape, jnp.int32),
            V(basis.shape, F32),
            V((1, DEG1), F32),
            V((8, 128), F32),
            V((8, 128), F32),
            V((24, 128), F32),
            V((24, 128), F32),
            V((WH, WG, 8, 128), F32),
            V((WH, WG, 24, 128), F32),
            V((L // 128, 4 * XP * 8, 128), F32),
            V((2, XP, L), F32),
            V((L // 128, XP * 24, 128), F32),
            V((L // 128, XP * 8, 128), F32),
            V((NE, NODES), F32),
            V((NE, NODES), F32),
            V((NODES, NODES), BF16),
            V((NODES, NODES), BF16),
            V((NODES, NODES), BF16),
            V((NODES, NODES), BF16),
            V((2, 16, NODES), F32),
            V((2, 16, NODES), F32),
            V((2, 16, NODES), F32),
            V((2, 16, NODES), F32),
            V((2, LY * LZ, NODES), F32),
            V((NE, NODES), F32),
            pltpu.SemaphoreType.DMA((5,)),
            pltpu.SemaphoreType.DMA((n_peers,)),
            pltpu.SemaphoreType.DMA((n_peers,)),
            pltpu.SemaphoreType.DMA((n_peers,)),
            pltpu.SemaphoreType.DMA((n_peers,)),
            pltpu.SemaphoreType.DMA((4,)),
            pltpu.SemaphoreType.DMA((4,)),
            pltpu.SemaphoreType.DMA((6,)),
            pltpu.SemaphoreType.DMA((6,)),
        ],
        compiler_params=pltpu.CompilerParams(
            collective_id=0, has_side_effects=True, vmem_limit_bytes=60 * 1024 * 1024
        ),
    )(rhs, coeff, flags, basis, eigenvalues.reshape(1, DEG1))
    return out.reshape(rhs.shape)


def solution(mesh):
    n_grp, n_gx, n_yz = (mesh.shape[a] for a in ("grp", "gx", "yz"))

    def call(rhs, coeff, flags, basis, eigenvalues):
        EX, EY, EZ = rhs.shape[:3]
        LX, LY, LZ = EX // n_gx, EY // n_yz, EZ // n_grp
        assert LX <= 3 and LY <= 4 and EZ <= 8 and n_grp <= 2

        def reach(steps, local, count):
            return min(-(-steps // local), count - 1)

        RG, RH = reach(REACH, LX, n_gx), reach(REACH, LY, n_yz)
        WG = n_gx if n_gx <= 2 * RG + 1 else 2 * RG + 1
        WH = n_yz if n_yz <= 2 * RH + 1 else 2 * RH + 1
        cfg = (n_grp, n_gx, n_yz, LX, LY, LZ, WG, WH, RG, RH)
        spec = (P("gx", "yz", "grp", None), P("gx", "yz", "grp"), P("gx", "yz", "grp"), P(), P())
        run = jax.shard_map(
            functools.partial(body, cfg), mesh=mesh, in_specs=spec,
            out_specs=P("gx", "yz", "grp", None), check_vma=False,
        )
        return run(rhs, coeff, flags, basis, eigenvalues)

    return call
```

```python
import functools

import jax
import jax.numpy as jnp
import numpy as np
from jax import lax
from jax.experimental import pallas as pl
from jax.experimental.pallas import tpu as pltpu
from jax.sharding import PartitionSpec as P

DEG1 = 8
NODES = 512
CHEB = 4
CHEB_LOW = 0.1
CHEB_HIGH = 2.0
REACH = 7
REACH_FACE = 4
GLL_POINTS = (
    -1.0,
    -0.8717401485096066,
    -0.5917001814331423,
    -0.2092992179024789,
    0.2092992179024789,
    0.5917001814331423,
    0.8717401485096066,
    1.0,
)
L0 = [(1.0 - x) * 0.5 for x in GLL_POINTS]
L1 = [(1.0 + x) * 0.5 for x in GLL_POINTS]
MASS_SAME = sum(a * a for a in L0)
MASS_OTHER = sum(a * b for a, b in zip(L0, L1))
MESH = pl.DeviceIdType.MESH
F32 = jnp.float32
BF16 = jnp.bfloat16


def iota(shape, dim):
    return lax.broadcasted_iota(jnp.int32, shape, dim)


def parts_of(x, count):
    found = []
    for _ in range(count):
        head = x.astype(BF16)
        found.append(head)
        x = x - head.astype(F32)
    return found


def dot(a, b, dims=((1,), (0,)), parts=(2, 2)):
    pa, pb = parts_of(a, parts[0]), parts_of(b, parts[1])
    order = max(parts)
    out = None
    for p in range(parts[0]):
        for q in range(parts[1]):
            if p + q < order:
                term = lax.dot_general(pa[p], pb[q], (dims, ((), ())), preferred_element_type=F32)
                out = term if out is None else out + term
    return out


def split(x):
    hi = x.astype(BF16)
    return hi, (x - hi.astype(F32)).astype(BF16)


def dot3(x, hi, lo):
    xh, xl = split(x)
    rows = x.shape[0]
    both = jnp.dot(jnp.concatenate([xh, xl], axis=0), hi, preferred_element_type=F32)
    return both[:rows] + (both[rows:] + jnp.dot(xh, lo, preferred_element_type=F32))


def pick(index, table):
    out = jnp.full(index.shape, table[0], F32)
    for i in range(1, len(table)):
        out = jnp.where(index == i, table[i], out)
    return out


def kernel(
    cfg,
    rhs_hbm, coeff_hbm, flags_hbm, basis_hbm, eig_hbm,
    out_ref,
    rhs_ref, coeff_ref, flags_ref, basis_ref, eig_ref,
    mine_b, other_b, mine_p, other_p, win_b, win_p, planes, cfx, ext3, ext1,
    rhs_s, s_ref, e_hi, e_lo, t_hi, t_lo,
    ysend, yrecv, zsend, zrecv, xrecv, nb,
    in_sem, b_send, b_recv, p_send, p_recv, g_send, g_recv, fsend, frecv,
):
    n_grp, n_gx, n_yz, LX, LY, LZ, WG, WH, RG, RH = cfg
    LT = planes.shape[0]
    L = LT * 128
    XP = cfx.shape[1]
    FROWS = XP * 8
    me_grp = lax.axis_index("grp")
    me_gx = lax.axis_index("gx")
    me_yz = lax.axis_index("yz")
    full_g = WG == n_gx
    full_h = WH == n_yz
    gs = me_gx if full_g else RG
    hs = me_yz if full_h else RH
    g_start = 0 if full_g else me_gx - RG
    h_start = 0 if full_h else me_yz - RH

    loads = []
    pairs_in = [
        (basis_hbm, basis_ref), (eig_hbm, eig_ref), (rhs_hbm, rhs_ref),
        (coeff_hbm, coeff_ref), (flags_hbm, flags_ref),
    ]
    for n, (src, dst) in enumerate(pairs_in):
        load = pltpu.make_async_copy(src, dst, in_sem.at[n])
        load.start()
        loads.append(load)
    win_b[...] = jnp.zeros(win_b.shape, F32)
    win_p[...] = jnp.zeros(win_p.shape, F32)

    me_of = {"grp": me_grp, "gx": me_gx, "yz": me_yz}
    n_of = {"grp": n_grp, "gx": n_gx, "yz": n_yz}

    def exists(axis, k):
        at = me_of[axis] + k
        return jnp.logical_and(at >= 0, at < n_of[axis])

    def cost(k, local):
        return 0 if k == 0 else (abs(k) - 1) * local + 1

    def around(reach):
        return [
            (kg, kh)
            for kg in range(-RG, RG + 1)
            for kh in range(-RH, RH + 1)
            if (kg, kh) != (0, 0) and cost(kg, LX) + cost(kh, LY) <= reach
        ]

    def target(key):
        return {axis: me_of[axis] + k for axis, k in key if k}

    def present(key):
        there = None
        for axis, k in key:
            if k:
                here = exists(axis, k)
                there = here if there is None else jnp.logical_and(there, here)
        return there

    grp_keys = [(("grp", k),) for k in (-1, 1)] if n_grp > 1 else []
    b_keys = [(("gx", kg), ("yz", kh)) for kg, kh in around(REACH)]
    p_keys = [(("gx", kg), ("yz", kh)) for kg, kh in around(REACH_FACE)]

    barrier = pltpu.get_barrier_semaphore()
    count = jnp.int32(0)
    for key in grp_keys + b_keys:
        here = present(key)
        count = count + here.astype(jnp.int32)

        @pl.when(here)
        def _(key=key):
            pl.semaphore_signal(barrier, inc=1, device_id=target(key), device_id_type=MESH)

    lane = iota((8, NODES), 1)
    sub = iota((8, NODES), 0)
    v1 = (lane // 64 == sub).astype(F32)
    v2 = ((lane // 8) % 8 == sub).astype(F32)
    v3 = (lane % 8 == sub).astype(F32)

    node_at = (lane // 64, (lane // 8) % 8, lane % 8)
    side_at = (sub // 4, (sub // 2) % 2, sub % 2)
    restrict = jnp.ones((8, NODES), F32)
    for d in range(3):
        restrict = restrict * jnp.where(side_at[d] == 0, pick(node_at[d], L0), pick(node_at[d], L1))
    on_face = [
        jnp.where(node_at[d] == 7 * side_at[d], restrict, 0.0) for d in range(3)
    ]
    faces = jnp.concatenate(on_face, axis=0)

    YZ = LY * LZ
    NE = LX * YZ
    row = iota((NE, 1), 0)
    row_x, row_y, row_z = row // YZ, (row // LZ) % LY, row % LZ
    ysel = (iota((YZ, LY), 0) // LZ == iota((YZ, LY), 1)).astype(F32)
    zsel = iota((YZ, LZ), 0) % LZ == iota((YZ, LZ), 1)

    r16 = iota((YZ, 128), 0)
    l16 = iota((YZ, 128), 1)
    spot = (r16 // LZ) * 8 + me_grp * LZ + r16 % LZ
    tail = (l16 == 96 + spot).astype(F32)
    re = iota((NE, 128), 0)
    place = (
        iota((NE, 128), 1) == (re // YZ) * 32 + ((re // LZ) % LY) * 8 + me_grp * LZ + re % LZ
    ).astype(F32)

    for load in loads[2:]:
        load.wait()
    for x in range(LX):
        for y in range(LY):
            at = x * YZ + y * LZ
            rhs_s[at : at + LZ, :] = rhs_ref[x, y]
    rhs = rhs_s[...]
    def column(ref):
        parts = []
        for x in range(LX):
            spread = dot(ysel, ref[x].astype(F32), parts=(1, 3))
            parts.append(jnp.sum(jnp.where(zsel, spread, 0.0), axis=1, keepdims=True))
        return parts

    coeff_cols = column(coeff_ref)
    flag_cols = column(flags_ref)
    coeff_col = jnp.concatenate(coeff_cols, axis=0)
    flag_col = jnp.concatenate(flag_cols, axis=0)

    b_own = dot(dot(restrict, rhs, ((1,), (1,))), place, parts=(2, 1))
    row8 = iota((8, 128), 0)
    for x in range(LX):
        c_line = jnp.sum(coeff_cols[x] * tail, axis=0, keepdims=True)
        f_line = jnp.sum(flag_cols[x] * tail, axis=0, keepdims=True)
        b_own = b_own + jnp.where(row8 == x, c_line, 0.0) + jnp.where(row8 == LX + x, f_line, 0.0)
    mine_b[...] = b_own

    def remote(src, dst, send, recv, n, key):
        copy = pltpu.make_async_remote_copy(
            src_ref=src, dst_ref=dst, send_sem=send.at[n], recv_sem=recv.at[n],
            device_id=target(key), device_id_type=MESH,
        )
        return key, copy

    def around_copies(ref, keys, send, recv):
        found = []
        for n, key in enumerate(keys):
            kg, kh = key[0][1], key[1][1]
            slot = (hs if full_h else RH - kh, gs if full_g else RG - kg)
            found.append(remote(ref.at[hs, gs], ref.at[slot[0], slot[1]], send, recv, n, key))
        return found

    def start_all(copies):
        for key, copy in copies:
            @pl.when(present(key))
            def _(copy=copy):
                copy.start()

    def wait_recv(copies):
        for key, copy in copies:
            @pl.when(present([(axis, -k) for axis, k in key]))
            def _(copy=copy):
                copy.wait_recv()

    def wait_send(copies):
        for key, copy in copies:
            @pl.when(present(key))
            def _(copy=copy):
                copy.wait_send()

    grp_b = [remote(mine_b, other_b, g_send, g_recv, n, key) for n, key in enumerate(grp_keys)]
    grp_p = [remote(mine_p, other_p, g_send, g_recv, 2 + n, key) for n, key in enumerate(grp_keys)]
    all_b = around_copies(win_b, b_keys, b_send, b_recv)
    all_p = around_copies(win_p, p_keys, p_send, p_recv)

    pl.semaphore_wait(barrier, count)
    start_all(grp_b)
    loads[0].wait()
    loads[1].wait()
    basis = basis_ref[...]

    def build(hi_ref, lo_ref, dims):
        t1 = dot(basis, v1, dims, (3, 1))
        t2 = dot(basis, v2, dims, (3, 1))
        t3 = dot(basis, v3, dims, (3, 1))
        pairs = jnp.concatenate([t2[j : j + 1, :] * t3 for j in range(8)], axis=0)
        for i in range(8):
            hi, lo = split(t1[i : i + 1, :] * pairs)
            hi_ref[i * 64 : (i + 1) * 64, :] = hi
            lo_ref[i * 64 : (i + 1) * 64, :] = lo

    build(e_hi, e_lo, ((1,), (0,)))
    build(t_hi, t_lo, ((0,), (0,)))
    spectrum = dot(eig_ref[...], v1 + v2 + v3, parts=(3, 1))

    inverse = 1.0 / (coeff_col * spectrum)
    wait_recv(grp_b)
    win_b[hs, gs] = mine_b[...] + other_b[...] if n_grp > 1 else mine_b[...]
    start_all(all_b)
    s = dot3(dot3(rhs, e_hi[...], e_lo[...]) * inverse, t_hi[...], t_lo[...])
    s_ref[...] = s
    mine_p[...] = dot(dot(faces, s, ((1,), (1,))), place, parts=(2, 1))
    start_all(grp_p)

    for side in range(2):
        yy, zz = (0, 0) if side == 0 else (LY - 1, LZ - 1)
        for x in range(LX):
            ysend[side, x * LZ : (x + 1) * LZ, :] = s_ref[x * YZ + yy * LZ : x * YZ + (yy + 1) * LZ, :]
            for y in range(LY):
                at = x * YZ + y * LZ + zz
                zsend[side, x * LY + y : x * LY + y + 1, :] = s_ref[at : at + 1, :]

    def face_copies():
        found = []
        for n, (axis, k) in enumerate(
            [("gx", -1), ("gx", 1), ("yz", -1), ("yz", 1), ("grp", -1), ("grp", 1)]
        ):
            if n_of[axis] == 1:
                continue
            side = 0 if k < 0 else 1
            if axis == "gx":
                at = 0 if side == 0 else (LX - 1) * YZ
                src, dst = s_ref.at[pl.ds(at, YZ)], xrecv.at[1 - side]
            elif axis == "yz":
                src, dst = ysend.at[side], yrecv.at[1 - side]
            else:
                src, dst = zsend.at[side], zrecv.at[1 - side]
            found.append(remote(src, dst, fsend, frecv, n, ((axis, k),)))
        return found

    next_door = face_copies()
    start_all(next_door)
    wait_recv(grp_p)
    win_p[hs, gs] = mine_p[...] + other_p[...] if n_grp > 1 else mine_p[...]
    start_all(all_p)
    planes[...] = jnp.zeros(planes.shape, F32)
    cfx[...] = jnp.zeros(cfx.shape, F32)
    wait_recv(next_door)

    own_at = (me_gx * LX + row_x, me_yz * LY + row_y, me_grp * LZ + row_z)
    totals = (n_gx * LX, n_yz * LY, n_grp * LZ)
    node_lane = iota((1, NODES), 1)
    node_of = (node_lane // 64, (node_lane // 8) % 8, node_lane % 8)
    strides = (64, 8, 1)
    face_s = jnp.zeros((NE, NODES), F32)
    for d in range(3):
        for side in range(2):
            if d == 0:
                if side == 0:
                    beside = jnp.concatenate([xrecv[0], s[: NE - YZ]], axis=0)
                else:
                    beside = jnp.concatenate([s[YZ:], xrecv[1]], axis=0)
            else:
                step = LZ if d == 1 else 1
                nb[...] = pltpu.roll(s, step if side == 0 else NE - step, 0)
                for x in range(LX):
                    if d == 1:
                        at = x * YZ + (0 if side == 0 else (LY - 1) * LZ)
                        nb[at : at + LZ, :] = yrecv[side, x * LZ : (x + 1) * LZ, :]
                    else:
                        for y in range(LY):
                            at = x * YZ + y * LZ + (0 if side == 0 else LZ - 1)
                            nb[at : at + 1, :] = zrecv[side, x * LY + y : x * LY + y + 1, :]
                beside = nb[...]
            has = own_at[d] > 0 if side == 0 else own_at[d] < totals[d] - 1
            gain = jnp.where(has, 1.0, flag_col)
            shift = 7 * strides[d]
            moved = pltpu.roll(beside, NODES - shift if side == 0 else shift, 1)
            term = gain * s - jnp.where(has, moved, 0.0)
            face_s = face_s + jnp.where(node_of[d] == 7 * side, term, 0.0)

    wait_recv(all_b)

    def spread(win, rows, first_field):
        lane_slot = iota((rows, L), 1) // 32
        for g in range(WG):
            cf_plane = jnp.zeros((rows, L), F32)
            tiles = []
            for h in range(WH):
                tile = win[h, g]
                if L > 128:
                    tile = jnp.concatenate([tile, jnp.zeros((rows, L - 128), F32)], axis=1)
                tiles.append(tile)
                if first_field == 0:
                    moved = pltpu.roll(tile, (32 * (h - 3)) % L, 1)
                    cf_plane = jnp.where(lane_slot == h, moved, cf_plane)
            for x in range(LX):
                plane = jnp.zeros((rows, L), F32)
                for h in range(WH):
                    amount = (32 * (h - x)) % L
                    moved = pltpu.roll(tiles[h], amount, 1) if amount else tiles[h]
                    plane = jnp.where(lane_slot == h, moved, plane)
                at = (g * LX + x) * 8
                for f in range(rows // 8):
                    to = (first_field + f) * FROWS + at
                    for t in range(LT):
                        part = plane[f * 8 : f * 8 + 8, t * 128 : (t + 1) * 128]
                        planes[t, to : to + 8, :] = part
            if first_field == 0:
                cfx[0, g * LX : (g + 1) * LX, :] = cf_plane[0:LX]
                cfx[1, g * LX : (g + 1) * LX, :] = cf_plane[LX : 2 * LX]

    spread(win_b, 8, 0)

    def strided(ref, start, stride):
        parts = [ref[t, pl.ds(start, XP, stride=stride), :] for t in range(LT)]
        return parts[0] if LT == 1 else jnp.concatenate(parts, axis=1)

    def store_strided(ref, start, stride, value):
        for t in range(LT):
            ref[t, pl.ds(start, XP, stride=stride), :] = value[:, t * 128 : (t + 1) * 128]

    def field(f):
        return [strided(planes, f * FROWS + a, 8) for a in range(8)]

    rhs1 = field(0)
    coeff = cfx[0]
    flag = cfx[1]
    pos = (
        g_start * LX + iota((XP, L), 0),
        h_start * LY + iota((XP, L), 1) // 8,
        iota((XP, L), 1) % 8,
    )
    has = [(pos[d] > 0, pos[d] < totals[d] - 1) for d in range(3)]
    gain = [[jnp.where(has[d][q], 1.0, flag) for q in range(2)] for d in range(3)]
    roll_axis = (0, 1, 1)
    roll_step = (1, 8, 1)
    bit = (4, 2, 1)

    def side_of(a, d):
        return (a // bit[d]) % 2

    def beside_of(v, a, d):
        q = side_of(a, d)
        size = XP if d == 0 else L
        step = roll_step[d] if q == 0 else size - roll_step[d]
        return jnp.where(has[d][q], pltpu.roll(v[a ^ bit[d]], step, roll_axis[d]), 0.0)

    def jump(v, a, d):
        return gain[d][side_of(a, d)] * v[a] - beside_of(v, a, d)

    diag = [
        coeff * 3.5 + gain[0][side_of(a, 0)] + gain[1][side_of(a, 1)] + gain[2][side_of(a, 2)]
        for a in range(8)
    ]

    def coarse_apply(v):
        out = []
        for a in range(8):
            flips = v[a ^ 4] + v[a ^ 2] + v[a ^ 1]
            sides = beside_of(v, a, 0) + beside_of(v, a, 1) + beside_of(v, a, 2)
            out.append(diag[a] * v[a] - coeff * flips - sides)
        return out

    center = 0.5 * (CHEB_HIGH + CHEB_LOW)
    half_width = 0.5 * (CHEB_HIGH - CHEB_LOW)
    inverse_diag = 1.0 / (coeff * 3.5 + 3.0)

    def cheb(f):
        sigma = center / half_width
        rho = 1.0 / sigma
        remain = f
        first = inverse_diag * (1.0 / center)
        update = [first * r for r in remain]
        result = update
        for _ in range(CHEB - 1):
            applied = coarse_apply(update)
            remain = [r - t for r, t in zip(remain, applied)]
            rho_next = 1.0 / (2.0 * sigma - rho)
            weight = inverse_diag * (2.0 * rho_next / half_width)
            update = [(rho_next * rho) * u + weight * r for u, r in zip(update, remain)]
            result = [t + u for t, u in zip(result, update)]
            rho = rho_next
        return result

    col = iota((8, 8), 0)
    w = [jnp.sum(pick(col, t) * basis, axis=0, keepdims=True) for t in (L0, L1)]
    eig = eig_ref[...]
    stiff = [[jnp.sum(eig * w[p] * w[q], axis=1, keepdims=True) for q in range(2)] for p in range(2)]

    def mass(v, d):
        return [MASS_SAME * v[a] + MASS_OTHER * v[a ^ bit[d]] for a in range(8)]

    c1 = cheb(rhs1)
    m3 = mass(c1, 2)
    m23 = mass(m3, 1)
    m13 = mass(m3, 0)
    m12 = mass(mass(c1, 1), 0)
    masses = (m23, m13, m12)
    rhs2 = []
    for a in range(8):
        inner = 0.0
        for d in range(3):
            q = side_of(a, d)
            inner = inner + stiff[q][q] * masses[d][a] + stiff[q][1 - q] * masses[d][a ^ bit[d]]
        rhs2.append(0.5 * rhs1[a] - 0.5 * coeff * inner)
    first_row = gs * LX
    absolute = hs * 32 + (iota((YZ, L), 0) // LZ) * 8 + me_grp * LZ + iota((YZ, L), 0) % LZ
    take = (iota((YZ, L), 1) == absolute).astype(F32)

    def own_values(ref, comps):
        parts = []
        for x in range(LX):
            start = pl.multiple_of((first_row + x) * comps, 8)
            part = 0.0
            for t in range(LT):
                lanes = take[:, t * 128 : (t + 1) * 128]
                part = part + dot(lanes, ref[t, pl.ds(start, comps), :], ((1,), (1,)), (1, 2))
            parts.append(part)
        return jnp.concatenate(parts, axis=0)

    for d in range(3):
        for a in range(8):
            store_strided(ext3, d * 8 + a, 24, jump(c1, a, d))
    face_c = dot(own_values(ext3, 24), faces)
    total = face_s + face_c
    smooth2 = dot3(dot3(total, e_hi[...], e_lo[...]) * inverse, t_hi[...], t_lo[...])

    wait_recv(all_p)
    spread(win_p, 24, 1)
    proj = [field(1 + d) for d in range(3)]
    for d in range(3):
        both = [proj[d][a] + masses[d][a] for a in range(8)]
        rhs2 = [rhs2[a] - jump(both, a, d) for a in range(8)]
    c2 = cheb(rhs2)
    for a in range(8):
        store_strided(ext1, a, 8, 0.25 * c1[a] + 0.5 * c2[a])
    lifted = dot(own_values(ext1, 8), restrict)
    out_ref[...] = 0.75 * s + lifted - 0.5 * smooth2

    for copies in (grp_b, grp_p, all_b, all_p, next_door):
        wait_send(copies)


def body(cfg, rhs, coeff, flags, basis, eigenvalues):
    n_grp, n_gx, n_yz, LX, LY, LZ, WG, WH, RG, RH = cfg
    NE = LX * LY * LZ
    L = -(-(WH * 32) // 128) * 128
    XP = -(-(WG * LX) // 8) * 8
    V = pltpu.VMEM
    n_peers = (2 * RG + 1) * (2 * RH + 1)
    out = pl.pallas_call(
        functools.partial(kernel, cfg),
        out_shape=V((NE, NODES), F32),
        in_specs=[pl.BlockSpec(memory_space=pltpu.HBM)] * 5,
        out_specs=pl.BlockSpec(memory_space=V),
        scratch_shapes=[
            V(rhs.shape, F32),
            V(coeff.shape, F32),
            V(flags.shape, jnp.int32),
            V(basis.shape, F32),
            V((1, DEG1), F32),
            V((8, 128), F32),
            V((8, 128), F32),
            V((24, 128), F32),
            V((24, 128), F32),
            V((WH, WG, 8, 128), F32),
            V((WH, WG, 24, 128), F32),
            V((L // 128, 4 * XP * 8, 128), F32),
            V((2, XP, L), F32),
            V((L // 128, XP * 24, 128), F32),
            V((L // 128, XP * 8, 128), F32),
            V((NE, NODES), F32),
            V((NE, NODES), F32),
            V((NODES, NODES), BF16),
            V((NODES, NODES), BF16),
            V((NODES, NODES), BF16),
            V((NODES, NODES), BF16),
            V((2, 16, NODES), F32),
            V((2, 16, NODES), F32),
            V((2, 16, NODES), F32),
            V((2, 16, NODES), F32),
            V((2, LY * LZ, NODES), F32),
            V((NE, NODES), F32),
            pltpu.SemaphoreType.DMA((5,)),
            pltpu.SemaphoreType.DMA((n_peers,)),
            pltpu.SemaphoreType.DMA((n_peers,)),
            pltpu.SemaphoreType.DMA((n_peers,)),
            pltpu.SemaphoreType.DMA((n_peers,)),
            pltpu.SemaphoreType.DMA((4,)),
            pltpu.SemaphoreType.DMA((4,)),
            pltpu.SemaphoreType.DMA((6,)),
            pltpu.SemaphoreType.DMA((6,)),
        ],
        compiler_params=pltpu.CompilerParams(
            collective_id=0, has_side_effects=True, vmem_limit_bytes=60 * 1024 * 1024
        ),
    )(rhs, coeff, flags, basis, eigenvalues.reshape(1, DEG1))
    return out.reshape(rhs.shape)


def solution(mesh):
    n_grp, n_gx, n_yz = (mesh.shape[a] for a in ("grp", "gx", "yz"))

    def call(rhs, coeff, flags, basis, eigenvalues):
        EX, EY, EZ = rhs.shape[:3]
        LX, LY, LZ = EX // n_gx, EY // n_yz, EZ // n_grp
        assert LX <= 3 and LY <= 4 and EZ <= 8 and n_grp <= 2

        def reach(steps, local, count):
            return min(-(-steps // local), count - 1)

        RG, RH = reach(REACH, LX, n_gx), reach(REACH, LY, n_yz)
        WG = n_gx if n_gx <= 2 * RG + 1 else 2 * RG + 1
        WH = n_yz if n_yz <= 2 * RH + 1 else 2 * RH + 1
        cfg = (n_grp, n_gx, n_yz, LX, LY, LZ, WG, WH, RG, RH)
        spec = (P("gx", "yz", "grp", None), P("gx", "yz", "grp"), P("gx", "yz", "grp"), P(), P())
        run = jax.shard_map(
            functools.partial(body, cfg), mesh=mesh, in_specs=spec,
            out_specs=P("gx", "yz", "grp", None), check_vma=False,
        )
        return run(rhs, coeff, flags, basis, eigenvalues)

    return call
```
